128 devices in a mesh: row: 8 (over z, core), col: 16 (over x, y).
Axes of the slice: x: 4, y: 4, z: 4, core: 2. Of those that a mesh axis runs over, the one named last changes fastest.
Arguments:
- kernel: float32 [8192, 8192], P('row', 'col'), as said below
Outputs:
- factored: float32 [8192, 8192], P('row', 'col')
Inputs may be any that keep to these rules, and one draw needn't show every extreme that they name: kernel stores a symmetric positive definite matrix in the tile order of the steps.
All inputs are finite; a program needn't handle non-finite values.
Results may differ from the reference program's by a relative error of at most 0.0003.
Values sent between devices are 32-bit elements; how exact they have to be, the bound alone decides.
A program may use at most 128 MiB of HBM per device.

```python
import math
import jax
import jax.numpy as jnp
from jax import lax

TILE = 512
PANEL = 1024
TC_DEV = 1
TR_DEV = 2
ORDER = 8192
N_ROW = 8
N_COL = 16


def to_store_drawn(natural):
    rows_done = natural.reshape(TR_DEV, N_ROW, TILE, ORDER).transpose(1, 0, 2, 3).reshape(ORDER, ORDER)
    return rows_done.reshape(ORDER, TC_DEV, N_COL, TILE).transpose(0, 2, 1, 3).reshape(ORDER, ORDER)


def gaussian_gram(points, spread):
    distance = jnp.zeros((ORDER, ORDER), jnp.float32)
    for axis_pos in range(6):
        coordinate = points[:, axis_pos]
        difference = coordinate[:, None] - coordinate[None, :]
        distance = distance + difference * difference
    kernel_values = jnp.exp(distance * (-1.0 / 6.0))
    ridged = kernel_values + 0.5 * jnp.eye(ORDER, dtype=jnp.float32)
    return ridged * spread[:, None] * spread[None, :]


def draw_kernel(key, part):
    key = jax.random.fold_in(key, 11)
    key_points, key_scale = jax.random.split(key, 2)
    points = jax.random.normal(key_points, (ORDER, 6), jnp.float32)
    spread = jnp.exp(jax.random.uniform(key_scale, (ORDER,), jnp.float32, 0.0, math.log(2.0)))
    return to_store_drawn(gaussian_gram(points, spread))


def setup_inputs(seed: int = 0) -> dict:
    key_of = jax.random.split(jax.random.key(seed), 2)
    kernel = draw_kernel(jax.random.fold_in(key_of[1], 71), 0)
    return dict(kernel=kernel)


def from_store(stored):
    rows_done = stored.reshape(N_ROW, TR_DEV, TILE, ORDER).transpose(1, 0, 2, 3).reshape(ORDER, ORDER)
    return rows_done.reshape(ORDER, N_COL, TC_DEV, TILE).transpose(0, 2, 1, 3).reshape(ORDER, ORDER)

def to_store(natural):
    rows_done = natural.reshape(TR_DEV, N_ROW, TILE, ORDER).transpose(1, 0, 2, 3).reshape(ORDER, ORDER)
    return rows_done.reshape(ORDER, TC_DEV, N_COL, TILE).transpose(0, 2, 1, 3).reshape(ORDER, ORDER)

def reference(kernel):
    working = from_store(kernel)
    for panel_index in range(2):
        start_col = panel_index * PANEL
        end_col = start_col + PANEL
        factor = jnp.linalg.cholesky(working[start_col:end_col, start_col:end_col])
        below_rows = jax.scipy.linalg.solve_triangular(factor, working[end_col:, start_col:end_col].T, lower=True).T
        product = jnp.dot(below_rows.astype(jnp.float32), below_rows.T.astype(jnp.float32), precision=lax.Precision.HIGHEST, preferred_element_type=jnp.float32)
        working = working.at[end_col:, end_col:].add(-product)
        working = working.at[start_col:, start_col:end_col].set(jnp.concatenate([factor, below_rows], 0))
        working = working.at[start_col:end_col, end_col:].set(jnp.zeros((PANEL, ORDER - end_col), jnp.float32))
    return to_store(working)
```

```python
import functools

import jax
import jax.numpy as jnp
from jax import lax
from jax.experimental import pallas as pl
from jax.experimental.pallas import tpu as pltpu
from jax.sharding import PartitionSpec as P

T = 512
W = 1024
B = 128
H = 256
MESH = pl.DeviceIdType.MESH
NT = (((1,), (1,)), ((), ()))
NN = (((1,), (0,)), ((), ()))


def split(x):
    hi = x.astype(jnp.bfloat16)
    lo = (x - hi.astype(jnp.float32)).astype(jnp.bfloat16)
    return hi, lo


def dot3(a, b, dims=NT):
    (ah, al), (bh, bl) = a, b
    d = functools.partial(
        lax.dot_general, dimension_numbers=dims, preferred_element_type=jnp.float32
    )
    return d(ah, bh) + (d(ah, bl) + d(al, bh))


def lane(x, i):
    return jnp.broadcast_to(x[:, i : i + 1], (8, B))


def sub(x, i):
    return jnp.broadcast_to(x[i : i + 1, :], (8, B))


def chol_block(block):
    n = B // 8
    li = lax.broadcasted_iota(jnp.int32, (8, B), 1)
    si = lax.broadcasted_iota(jnp.int32, (8, B), 0)
    rows = [block[8 * i : 8 * i + 8] for i in range(n)]
    eye = [(li == si + 8 * i).astype(jnp.float32) for i in range(n)]
    upper, inverse = [], []

    def merge(xs):
        out = xs[0]
        for t in range(1, 8):
            out = jnp.where(si == t, xs[t], out)
        return out

    for j in range(n):
        o = 8 * j
        cols = [lane(rows[j], o + q) for q in range(8)]
        m = {(p, q): sub(cols[q], p) for q in range(8) for p in range(q, 8)}
        rb = [sub(rows[j], p) for p in range(8)]
        eb = [sub(eye[j], p) for p in range(8)]
        nxt = j + 1 < n
        if nxt:
            raw = [[lane(rows[i], o + q) for q in range(8)] for i in range(j + 1, n)]
            nc = list(raw[0])
        rk = [None] * 8
        fs = {}
        for k in range(8):
            rk[k] = 1.0 / m[k, k]
            for q in range(k + 1, 8):
                if q == k + 1:
                    m[q, q] = m[q, q] - (m[q, k] * m[q, k]) * rk[k]
                f = m[q, k] * rk[k]
                fs[q, k] = f
                for p in range(q + (1 if q == k + 1 else 0), 8):
                    m[p, q] = m[p, q] - m[p, k] * f
                rb[q] = rb[q] - f * rb[k]
                eb[q] = eb[q] - f * eb[k]
                if nxt:
                    nc[q] = nc[q] - f * nc[k]
            if nxt:
                c = nc[k] * rk[k]
                rows[j + 1] = rows[j + 1] - c * rb[k]
                eye[j + 1] = eye[j + 1] - c * eb[k]
        sk = lax.rsqrt(merge([m[k, k] for k in range(8)]))
        upper.append(merge(rb) * sk)
        inverse.append(merge(eb) * sk)
        if j + 2 < n:
            vr = [rb[k] * rk[k] for k in range(8)]
            ve = [eb[k] * rk[k] for k in range(8)]
            for q in range(7, -1, -1):
                for k in range(q):
                    vr[k] = vr[k] - fs[q, k] * vr[q]
                    ve[k] = ve[k] - fs[q, k] * ve[q]
            for i in range(j + 2, n):
                ar, ae = rows[i], eye[i]
                for q in range(8):
                    c = raw[i - j - 1][q]
                    ar = ar - c * vr[q]
                    ae = ae - c * ve[q]
                rows[i], eye[i] = ar, ae
    return jnp.concatenate(upper, 0), jnp.concatenate(inverse, 0)


def body(
    a_ref, m_ref, rbuf, cbuf, dbuf, lref, wref, lh, ll, wh, wl, xh, xl, uh, ul,
    ssem, r1, r2, r3, c1, c2, c3, d1, d2, d3, d4, d5, lsem,
):
    row = lax.axis_index("row")
    col = lax.axis_index("col")
    h = lax.rem(row, 2)
    z = lax.div(row, 2)
    x = lax.div(col, 4)
    y = lax.rem(col, 4)
    major = jnp.where(h == 0, x, y)
    minor = jnp.where(h == 0, y, x)
    mine = 4 * major + minor

    def col_of(ma, mi):
        return jnp.where(h == 0, 4 * ma + mi, 4 * mi + ma)

    def put(src, dst, send, recv, row_to, col_to):
        return pltpu.make_async_remote_copy(
            src_ref=src, dst_ref=dst, send_sem=send, recv_sem=recv,
            device_id=(row_to, col_to), device_id_type=MESH,
        )

    barrier = pltpu.get_barrier_semaphore()

    @pl.loop(1, 16)
    def _(t):
        pl.semaphore_signal(
            barrier, inc=1, device_id=(row, lax.rem(col + t, 16)), device_id_type=MESH
        )

    for t in range(1, 4):
        pl.semaphore_signal(
            barrier, inc=1, device_id=(2 * lax.rem(z + t, 4) + h, col), device_id_type=MESH
        )
    pl.semaphore_signal(barrier, inc=1, device_id=(2 * z + 1 - h, col), device_id_type=MESH)
    m_ref[...] = a_ref[...]
    pl.semaphore_wait(barrier, 19)

    def panel(p):
        first = 2 * p
        second = first + 1
        is_source = (x == 0) & ((y == first) | (y == second))
        half = jnp.where(y == second, 1, 0)
        mycols = pl.ds(pl.multiple_of(half * T, T), T)
        scols = [pl.ds(0, T), pl.ds(T, T)]
        R, C, D = rbuf.at[p], cbuf.at[p], dbuf.at[p]

        def rows(start, size):
            return pl.ds(pl.multiple_of(start * size, size), size)

        def d_rows(i, size):
            return pl.ds(pl.multiple_of(h * T + i * size, size), size)

        d_source = is_source & (z == p) & (half <= h)

        def d_scatter(i):
            return put(
                m_ref.at[rows(i, 32), :], D.at[d_rows(i, 32), mycols],
                ssem.at[p, 0, i], d1.at[p, half], row, col_of(lax.div(i, 4), lax.rem(i, 4)),
            )

        @pl.when(d_source)
        def _():
            @pl.loop(0, 16)
            def _(i):
                @pl.when(i != mine)
                def _():
                    d_scatter(i).start()

            own = pltpu.make_async_copy(
                m_ref.at[rows(mine, 32), :], D.at[d_rows(mine, 32), mycols], lsem.at[p, 0]
            )
            own.start()
            own.wait()

        def each_tile(cond, fn):
            for s in range(2):
                @pl.when(cond & (h >= s))
                def _():
                    fn(s)

        def d_from(s):
            put(
                m_ref.at[rows(mine, 32), :], D.at[d_rows(mine, 32), scols[s]],
                ssem.at[p, 0, 0], d1.at[p, s], row, col,
            ).wait_recv()

        for s in range(2):
            @pl.when((z == p) & (h >= s) & jnp.logical_not((x == 0) & (y == first + s)))
            def _():
                d_from(s)

        def d_z(s, t):
            ref = D.at[d_rows(mine, 32), scols[s]]
            return put(
                ref, ref, ssem.at[p, 1, s * 3 + t - 1], d2.at[p, s], 2 * lax.rem(z + t, 4) + h, col
            )

        def d_minor(s, t):
            ref = D.at[d_rows(mine, 32), scols[s]]
            return put(
                ref, ref, ssem.at[p, 2, s * 3 + t - 1], d3.at[p, s * 3 + t - 1],
                row, col_of(major, lax.rem(minor + t, 4)),
            )

        def d_minor_in(s, t):
            ref = D.at[d_rows(4 * major + lax.rem(minor + 4 - t, 4), 32), scols[s]]
            put(ref, ref, ssem.at[p, 2, 0], d3.at[p, s * 3 + t - 1], row, col).wait_recv()

        def d_major(s, t):
            ref = D.at[d_rows(major, 128), scols[s]]
            return put(
                ref, ref, ssem.at[p, 3, s * 3 + t - 1], d4.at[p, s * 3 + t - 1],
                row, col_of(lax.rem(major + t, 4), minor),
            )

        def d_major_in(s, t):
            ref = D.at[d_rows(lax.rem(major + 4 - t, 4), 128), scols[s]]
            put(ref, ref, ssem.at[p, 3, 0], d4.at[p, s * 3 + t - 1], row, col).wait_recv()

        def d_core(s):
            ref = D.at[pl.ds(pl.multiple_of(h * T, T), T), scols[s]]
            return put(ref, ref, ssem.at[p, 4, s], d5.at[p, s], 2 * z + 1 - h, col)

        def d_core_in(s):
            ref = D.at[pl.ds(pl.multiple_of((1 - h) * T, T), T), scols[s]]
            put(ref, ref, ssem.at[p, 4, 0], d5.at[p, s], row, col).wait_recv()

        each_tile(z == p, lambda s: [d_z(s, t).start() for t in (1, 2, 3)])
        each_tile(z != p, lambda s: d_z(s, 1).wait_recv())
        each_tile(z >= 0, lambda s: [d_minor(s, t).start() for t in (1, 2, 3)])
        each_tile(z >= 0, lambda s: [d_minor_in(s, t) for t in (1, 2, 3)])
        each_tile(z >= 0, lambda s: [d_major(s, t).start() for t in (1, 2, 3)])
        each_tile(z >= 0, lambda s: [d_major_in(s, t) for t in (1, 2, 3)])
        each_tile(z >= 0, lambda s: d_core(s).start())
        for s in range(2):
            @pl.when(1 - h >= s)
            def _():
                d_core_in(s)

        def r_scatter(i):
            return put(
                m_ref.at[rows(i, 64), :], R.at[rows(i, 64), mycols],
                ssem.at[p, 5, i], r1.at[p, half], row, col_of(lax.div(i, 4), lax.rem(i, 4)),
            )

        def r_minor(t):
            ref = R.at[rows(mine, 64), :]
            return put(
                ref, ref, ssem.at[p, 6, t - 1], r2.at[p, t - 1],
                row, col_of(major, lax.rem(minor + t, 4)),
            )

        def r_minor_in(t):
            ref = R.at[rows(4 * major + lax.rem(minor + 4 - t, 4), 64), :]
            put(ref, ref, ssem.at[p, 6, 0], r2.at[p, t - 1], row, col).wait_recv()

        def r_major(t):
            ref = R.at[rows(major, 256), :]
            return put(
                ref, ref, ssem.at[p, 7, t - 1], r3.at[p, t - 1],
                row, col_of(lax.rem(major + t, 4), minor),
            )

        def r_major_in(t):
            ref = R.at[rows(lax.rem(major + 4 - t, 4), 256), :]
            put(ref, ref, ssem.at[p, 7, 0], r3.at[p, t - 1], row, col).wait_recv()

        def c_rows(q):
            return pl.ds(pl.multiple_of(h * T + q * B, B), B)

        def c_first(t, which):
            zt = lax.rem(z + t, 4)
            q = zt if which == 0 else z
            return put(
                m_ref.at[rows(q, B), :], C.at[c_rows(q), :],
                ssem.at[p, 8, 2 * (t - 1) + which], c1.at[p, which], 2 * zt + h, col,
            )

        def c_first_in(which):
            q = z if which == 0 else p
            ref = C.at[c_rows(q), :]
            put(ref, ref, ssem.at[p, 8, 0], c1.at[p, which], row, col).wait_recv()

        def c_second(t):
            ref = C.at[c_rows(z), :]
            return put(
                ref, ref, ssem.at[p, 9, t - 1], c2.at[p, t - 1], 2 * lax.rem(z + t, 4) + h, col
            )

        def c_second_in(t):
            ref = C.at[c_rows(lax.rem(z + 4 - t, 4)), :]
            put(ref, ref, ssem.at[p, 9, 0], c2.at[p, t - 1], row, col).wait_recv()

        def c_core():
            ref = C.at[pl.ds(pl.multiple_of(h * T, T), T), :]
            return put(ref, ref, ssem.at[p, 10, 0], c3.at[p, 0], 2 * z + 1 - h, col)

        def c_core_in():
            ref = C.at[pl.ds(pl.multiple_of((1 - h) * T, T), T), :]
            put(ref, ref, ssem.at[p, 10, 0], c3.at[p, 0], row, col).wait_recv()

        def stage0():
            @pl.when(is_source)
            def _():
                @pl.loop(0, 16)
                def _(i):
                    @pl.when(i != mine)
                    def _():
                        r_scatter(i).start()

                own = pltpu.make_async_copy(
                    m_ref.at[rows(mine, 64), :], R.at[rows(mine, 64), mycols], lsem.at[p, 1]
                )
                own.start()
                own.wait()

            @pl.when(z == p)
            def _():
                for t in (1, 2, 3):
                    for which in (0, 1):
                        c_first(t, which).start()
                own = pltpu.make_async_copy(
                    m_ref.at[pl.ds(0, T), :],
                    C.at[pl.ds(pl.multiple_of(h * T, T), T), :], lsem.at[p, 2],
                )
                own.start()
                own.wait()

        def stage1():
            for s in range(2):
                @pl.when(jnp.logical_not((x == 0) & (y == first + s)))
                def _():
                    put(
                        m_ref.at[rows(mine, 64), :], R.at[rows(mine, 64), scols[s]],
                        ssem.at[p, 5, 0], r1.at[p, s], row, col,
                    ).wait_recv()
            for t in (1, 2, 3):
                r_minor(t).start()

            @pl.when(z != p)
            def _():
                c_first_in(0)
                for t in (1, 2, 3):
                    @pl.when(lax.rem(z + t, 4) != p)
                    def _():
                        c_second(t).start()
                c_first_in(1)

        def stage2():
            for t in (1, 2, 3):
                r_minor_in(t)
            for t in (1, 2, 3):
                r_major(t).start()

            @pl.when(z != p)
            def _():
                for t in (1, 2, 3):
                    @pl.when(lax.rem(z + 4 - t, 4) != p)
                    def _():
                        c_second_in(t)

            c_core().start()

        def stage3():
            for t in (1, 2, 3):
                r_major_in(t)
            c_core_in()

        def drain_d():
            @pl.when(d_source)
            def _():
                @pl.loop(0, 16)
                def _(i):
                    @pl.when(i != mine)
                    def _():
                        d_scatter(i).wait_send()

            each_tile(z == p, lambda s: [d_z(s, t).wait_send() for t in (1, 2, 3)])
            each_tile(z >= 0, lambda s: [d_minor(s, t).wait_send() for t in (1, 2, 3)])
            each_tile(z >= 0, lambda s: [d_major(s, t).wait_send() for t in (1, 2, 3)])
            each_tile(z >= 0, lambda s: d_core(s).wait_send())

        def drain_rc():
            @pl.when(is_source)
            def _():
                @pl.loop(0, 16)
                def _(i):
                    @pl.when(i != mine)
                    def _():
                        r_scatter(i).wait_send()

            for t in (1, 2, 3):
                r_minor(t).wait_send()
                r_major(t).wait_send()

            @pl.when(z == p)
            def _():
                for t in (1, 2, 3):
                    for which in (0, 1):
                        c_first(t, which).wait_send()

            @pl.when(z != p)
            def _():
                for t in (1, 2, 3):
                    @pl.when(lax.rem(z + t, 4) != p)
                    def _():
                        c_second(t).wait_send()

            c_core().wait_send()

        stage0()
        drain_d()

        lref[...] = jnp.zeros_like(lref)
        nb = W // B

        @pl.loop(0, nb)
        def _(k):
            o = pl.multiple_of(k * B, B)

            @pl.when(k == 1)
            def _():
                stage1()

            @pl.when(k == 3)
            def _():
                stage2()

            upper, inverse = chol_block(D[pl.ds(o, B), pl.ds(o, B)])
            wref[pl.ds(o, B), :] = inverse
            ri = lax.broadcasted_iota(jnp.int32, (B, B), 0)
            ci = lax.broadcasted_iota(jnp.int32, (B, B), 1)
            lref[pl.ds(o, B), pl.ds(o, B)] = jnp.where(ri >= ci, upper.T, 0.0)
            for kk in range(nb - 1):
                @pl.when(k == kk)
                def _():
                    s, e = kk * B, kk * B + B
                    xk = dot3(split(D[e:, s:e]), split(inverse))
                    lref[e:, s:e] = xk
                    xs = split(xk)
                    for c0 in range(e, W, H):
                        c1_ = min(c0 + H, W)
                        left = (xs[0][c0 - e :], xs[1][c0 - e :])
                        right = (xs[0][c0 - e : c1_ - e], xs[1][c0 - e : c1_ - e])
                        D[c0:, c0:c1_] = D[c0:, c0:c1_] - dot3(left, right)

        for g in range(4):
            w0 = wref[g * H : g * H + B, :]
            w1 = wref[g * H + B : g * H + H, :]
            l10 = lref[g * H + B : g * H + H, g * H : g * H + B]
            low = dot3(split(w1), split(dot3(split(l10), split(w0), NN)), NN)
            big = jnp.concatenate(
                [
                    jnp.concatenate([w0, jnp.zeros_like(w0)], 1),
                    jnp.concatenate([-low, w1], 1),
                ],
                0,
            )
            wh[g], wl[g] = split(big)

        @pl.loop(0, 4)
        def _(g):
            rs = rows(g, H)
            a, b = split(lref[rs, :])
            lh[rs, :] = a
            ll[rs, :] = b

        stage3()
        drain_rc()

        @pl.loop(0, 4)
        def _(g):
            rs = rows(g, H)
            for kb in range(4):
                ks = pl.ds(kb * H, H)
                xk = dot3(split(R[rs, ks]), (wh[kb], wl[kb]))
                R[rs, ks] = xk
                xs = split(xk)
                xh[rs, ks], xl[rs, ks] = xs
                for jb in range(kb + 1, 4):
                    js = pl.ds(jb * H, H)
                    R[rs, js] = R[rs, js] - dot3(xs, (lh[js, ks], ll[js, ks]))

        @pl.loop(0, 2)
        def _(g):
            cs = rows(g, H)
            for kb in range(4):
                ks = pl.ds(kb * H, H)
                us = split(dot3((wh[kb], wl[kb]), split(C[ks, cs]), NN))
                uh[ks, cs], ul[ks, cs] = us
                for jb in range(kb + 1, 4):
                    js = pl.ds(jb * H, H)
                    C[js, cs] = C[js, cs] - dot3((lh[js, ks], ll[js, ks]), us, NN)

        right_of = col > second
        in_panel = (col == first) | (col == second)
        top_below = row > second
        top_band = (row == first) | (row == second)

        def update(g):
            rs = rows(g, H)
            for n in range(2):
                cs = pl.ds(n * H, H)
                m_ref[rs, cs] = m_ref[rs, cs] - dot3(
                    (xh[rs, :], xl[rs, :]), (uh[:, cs], ul[:, cs]), NN
                )

        pcols = pl.ds(pl.multiple_of(jnp.where(col == second, T, 0), T), T)

        @pl.when(right_of)
        def _():
            @pl.when(top_below)
            def _():
                pl.loop(0, 2)(update)

            @pl.when(top_band)
            def _():
                m_ref[0:T, :] = jnp.zeros((T, T), jnp.float32)

            pl.loop(2, 4)(update)

        @pl.when(in_panel)
        def _():
            @pl.when(top_below)
            def _():
                m_ref[0:T, :] = R[0:T, pcols]

            @pl.when(top_band)
            def _():
                band = pl.ds(pl.multiple_of(jnp.where(row == second, T, 0), T), T)
                m_ref[0:T, :] = lref[band, pcols]

            m_ref[T : 2 * T, :] = R[T : 2 * T, pcols]

    pl.loop(0, 2)(panel)


def local(kernel):
    f32, b16 = jnp.float32, jnp.bfloat16
    dma = pltpu.SemaphoreType.DMA
    return pl.pallas_call(
        body,
        out_shape=jax.ShapeDtypeStruct((W, T), f32),
        in_specs=[pl.BlockSpec(memory_space=pltpu.VMEM)],
        out_specs=pl.BlockSpec(memory_space=pltpu.VMEM),
        scratch_shapes=[
            pltpu.VMEM((2, W, W), f32),
            pltpu.VMEM((2, W, T), f32),
            pltpu.VMEM((2, W, W), f32),
            pltpu.VMEM((W, W), f32),
            pltpu.VMEM((W, B), f32),
            pltpu.VMEM((W, W), b16),
            pltpu.VMEM((W, W), b16),
            pltpu.VMEM((4, H, H), b16),
            pltpu.VMEM((4, H, H), b16),
            pltpu.VMEM((W, W), b16),
            pltpu.VMEM((W, W), b16),
            pltpu.VMEM((W, T), b16),
            pltpu.VMEM((W, T), b16),
            dma((2, 11, 16)),
            dma((2, 2)), dma((2, 3)), dma((2, 3)),
            dma((2, 2)), dma((2, 3)), dma((2, 1)),
            dma((2, 2)), dma((2, 2)), dma((2, 6)), dma((2, 6)), dma((2, 2)),
            dma((2, 3)),
        ],
        compiler_params=pltpu.CompilerParams(
            collective_id=0, has_side_effects=True, vmem_limit_bytes=60 * 1024 * 1024
        ),
        cost_estimate=pl.CostEstimate(
            flops=20_000_000_000, bytes_accessed=8_000_000, transcendentals=0
        ),
        name="two_panels",
    )(kernel)


def solution(mesh):
    return jax.shard_map(
        local,
        mesh=mesh,
        in_specs=(P("row", "col"),),
        out_specs=P("row", "col"),
        check_vma=False,
    )
```

```python
import functools

import jax
import jax.numpy as jnp
from jax import lax
from jax.experimental import pallas as pl
from jax.experimental.pallas import tpu as pltpu
from jax.sharding import PartitionSpec as P

T = 512
W = 1024
B = 128
H = 256
MESH = pl.DeviceIdType.MESH
NT = (((1,), (1,)), ((), ()))
NN = (((1,), (0,)), ((), ()))


def split(x):
    hi = x.astype(jnp.bfloat16)
    lo = (x - hi.astype(jnp.float32)).astype(jnp.bfloat16)
    return hi, lo


def dot3(a, b, dims=NT):
    (ah, al), (bh, bl) = a, b
    d = functools.partial(
        lax.dot_general, dimension_numbers=dims, preferred_element_type=jnp.float32
    )
    return d(ah, bh) + (d(ah, bl) + d(al, bh))


def lane(x, i):
    return jnp.broadcast_to(x[:, i : i + 1], (8, B))


def sub(x, i):
    return jnp.broadcast_to(x[i : i + 1, :], (8, B))


def chol_block(block):
    n = B // 8
    li = lax.broadcasted_iota(jnp.int32, (8, B), 1)
    si = lax.broadcasted_iota(jnp.int32, (8, B), 0)
    rows = [block[8 * i : 8 * i + 8] for i in range(n)]
    eye = [(li == si + 8 * i).astype(jnp.float32) for i in range(n)]
    upper, inverse = [], []

    def merge(xs):
        out = xs[0]
        for t in range(1, 8):
            out = jnp.where(si == t, xs[t], out)
        return out

    for j in range(n):
        o = 8 * j
        cols = [lane(rows[j], o + q) for q in range(8)]
        m = {(p, q): sub(cols[q], p) for q in range(8) for p in range(q, 8)}
        rb = [sub(rows[j], p) for p in range(8)]
        eb = [sub(eye[j], p) for p in range(8)]
        nxt = j + 1 < n
        if nxt:
            raw = [[lane(rows[i], o + q) for q in range(8)] for i in range(j + 1, n)]
            nc = list(raw[0])
        rk = [None] * 8
        fs = {}
        for k in range(8):
            rk[k] = 1.0 / m[k, k]
            for q in range(k + 1, 8):
                if q == k + 1:
                    m[q, q] = m[q, q] - (m[q, k] * m[q, k]) * rk[k]
                f = m[q, k] * rk[k]
                fs[q, k] = f
                for p in range(q + (1 if q == k + 1 else 0), 8):
                    m[p, q] = m[p, q] - m[p, k] * f
                rb[q] = rb[q] - f * rb[k]
                eb[q] = eb[q] - f * eb[k]
                if nxt:
                    nc[q] = nc[q] - f * nc[k]
            if nxt:
                c = nc[k] * rk[k]
                rows[j + 1] = rows[j + 1] - c * rb[k]
                eye[j + 1] = eye[j + 1] - c * eb[k]
        sk = lax.rsqrt(merge([m[k, k] for k in range(8)]))
        upper.append(merge(rb) * sk)
        inverse.append(merge(eb) * sk)
        if j + 2 < n:
            vr = [rb[k] * rk[k] for k in range(8)]
            ve = [eb[k] * rk[k] for k in range(8)]
            for q in range(7, -1, -1):
                for k in range(q):
                    vr[k] = vr[k] - fs[q, k] * vr[q]
                    ve[k] = ve[k] - fs[q, k] * ve[q]
            for i in range(j + 2, n):
                ar, ae = rows[i], eye[i]
                for q in range(8):
                    c = raw[i - j - 1][q]
                    ar = ar - c * vr[q]
                    ae = ae - c * ve[q]
                rows[i], eye[i] = ar, ae
    return jnp.concatenate(upper, 0), jnp.concatenate(inverse, 0)


def body(
    a_ref, m_ref, rbuf, cbuf, lw, dbuf, work, lref, wref, lh, ll, wh, wl, xh, xl, uh, ul,
    ssem, r1, r2, r3, r4, c0, c1, c2, c3, d1, d2, d3, d5, l4, tsem, lsem,
):
    row = lax.axis_index("row")
    col = lax.axis_index("col")
    h = lax.rem(row, 2)
    z = lax.div(row, 2)
    x = lax.div(col, 4)
    y = lax.rem(col, 4)
    major = jnp.where(h == 0, x, y)
    def put(src, dst, send, recv, row_to, col_to):
        return pltpu.make_async_remote_copy(
            src_ref=src, dst_ref=dst, send_sem=send, recv_sem=recv,
            device_id=(row_to, col_to), device_id_type=MESH,
        )

    def rows(start, size):
        return pl.ds(pl.multiple_of(start * size, size), size)

    barrier = pltpu.get_barrier_semaphore()

    def greet(row_to, col_to):
        pl.semaphore_signal(barrier, inc=1, device_id=(row_to, col_to), device_id_type=MESH)

    @pl.loop(1, 16)
    def _(t):
        greet(row, lax.rem(col + t, 16))
        greet(2 * z + 1 - h, lax.rem(col + t, 16))

    for t in range(1, 4):
        greet(2 * lax.rem(z + t, 4), col)
        greet(2 * lax.rem(z + t, 4) + 1, col)
    greet(2 * z + 1 - h, col)
    load = pltpu.make_async_copy(a_ref, m_ref, lsem.at[0, 2])
    load.start()

    @pl.when(h == 0)
    def _():
        lref[...] = jnp.zeros_like(lref)

    load.wait()
    pl.semaphore_wait(barrier, 37)

    def panel(p):
        first = 2 * p
        second = first + 1
        is_source = (x == 0) & ((y == first) | (y == second))
        root = (row == first) & (col == first)
        half = jnp.where(y == second, 1, 0)
        mycols = pl.ds(pl.multiple_of(half * T, T), T)
        scols = [pl.ds(0, T), pl.ds(T, T)]
        R, C, LW, D = rbuf.at[p], cbuf.at[p], lw.at[p], dbuf.at[p]
        other = 2 * z + 1 - h

        head = D.at[pl.ds(0, B), pl.ds(0, B)]
        parts = ((B, 32, T, 12), (T, 64, W, 8))

        def h_plane(t):
            return put(
                m_ref.at[pl.ds(0, B), pl.ds(0, B)], head, ssem.at[p, 5, t], d5.at[p, 0],
                row, lax.rem(col + t, 16),
            )

        def h_planes(t):
            return put(
                head, head, ssem.at[p, 2, t], d5.at[p, 1], 2 * lax.rem(z + t, 4) + h, col
            )

        def head_start():
            @pl.when(root)
            def _():
                @pl.loop(1, 16)
                def _(t):
                    h_plane(t).start()

                own = pltpu.make_async_copy(
                    m_ref.at[pl.ds(0, B), pl.ds(0, B)], head, lsem.at[p, 2]
                )
                own.start()
                own.wait()
                for t in (1, 2, 3):
                    h_planes(t).start()

        def head_wait():
            @pl.when(z == p)
            def _():
                @pl.when(jnp.logical_not(root))
                def _():
                    h_plane(1).wait_recv()
                    for t in (1, 2, 3):
                        h_planes(t).start()

            @pl.when(z != p)
            def _():
                h_planes(1).wait_recv()

        def d_owner(n):
            return (h == 0) & ((x >= 1) if n == 0 else (lax.rem(x, 2) == 1))

        def d_mine(n):
            return col - 4 if n == 0 else 2 * y + lax.div(x, 2)

        def d_col(n, i):
            return 4 + i if n == 0 else 4 + 8 * lax.rem(i, 2) + lax.div(i, 2)

        def d_piece(n, i):
            start, size, width, _c = parts[n]
            return D.at[pl.ds(pl.multiple_of(start + i * size, size), size), pl.ds(0, width)]

        def d_scatter(n, i, s):
            start, size, width, _c = parts[n]
            here = pl.ds(pl.multiple_of((start if n == 0 else 0) + i * size, size), size)
            there = pl.ds(pl.multiple_of(start + i * size, size), size)
            dst = D.at[there, pl.ds(0, T) if n == 0 else s]
            return put(
                m_ref.at[here, :], dst, ssem.at[p, n, i],
                d1.at[p, n + (half if n else 0)], 2 * z, d_col(n, i),
            )

        def d_source(n):
            return root if n == 0 else is_source & (row == second)

        def d_start(n):
            @pl.when(d_source(n))
            def _():
                @pl.loop(0, parts[n][3])
                def _(i):
                    d_scatter(n, i, mycols).start()

        def d_planes(n, t):
            ref = d_piece(n, d_mine(n))
            return put(
                ref, ref, ssem.at[p, 3 + n, t], d2.at[p, n], 2 * lax.rem(z + t, 4) + h, col
            )

        def d_spread(n, t):
            ref = d_piece(n, d_mine(n))
            return put(
                ref, ref, ssem.at[p, 6 + n, t], d3.at[p, n, d_mine(n)],
                row, lax.rem(col + t, 16),
            )

        def d_forward(n):
            @pl.when(d_owner(n))
            def _():
                @pl.when(z == p)
                def _():
                    for s in range(1 + n):
                        ref = D.at[
                            pl.ds(
                                pl.multiple_of(
                                    parts[n][0] + d_mine(n) * parts[n][1], 32
                                ),
                                parts[n][1],
                            ),
                            scols[s],
                        ]
                        put(ref, ref, ssem.at[p, n, 0], d1.at[p, n + s], row, col).wait_recv()
                    for t in (1, 2, 3):
                        d_planes(n, t).start()

                @pl.when(z != p)
                def _():
                    d_planes(n, 1).wait_recv()

                if n == 0:
                    @pl.loop(1, 16)
                    def _(t):
                        d_spread(n, t).start()
                else:
                    for t in (1, 3, 2):
                        e_row(t).start()

        def e_row(t):
            ref = d_piece(1, d_mine(1))
            return put(
                ref, ref, ssem.at[p, 7, t], d3.at[p, 1, lax.div(x, 2)],
                row, 4 * lax.rem(x + t, 4) + y,
            )

        def e_rows(of):
            return D.at[pl.ds(pl.multiple_of(T + of * 128, 128), 128), :]

        def e_column(t):
            ref = e_rows(y)
            return put(
                ref, ref, ssem.at[p, 7, 4 + t], d3.at[p, 1, 1 + t],
                row, 4 * x + lax.rem(y + t, 4),
            )

        def e_across():
            for i in range(2):
                @pl.when(x != 1 + 2 * i)
                def _():
                    ref = d_piece(1, 2 * y + i)
                    put(ref, ref, ssem.at[p, 7, 0], d3.at[p, 1, i], row, col).wait_recv()

            for t in (1, 3, 2):
                e_column(t).start()

        def e_gather():
            for t in (1, 3, 2):
                ref = e_rows(lax.rem(y + 4 - t, 4))
                put(ref, ref, ssem.at[p, 7, 0], d3.at[p, 1, 1 + t], row, col).wait_recv()

        def d_gather(n):
            @pl.loop(0, parts[n][3])
            def _(i):
                @pl.when(col != d_col(n, i))
                def _():
                    ref = d_piece(n, i)
                    put(
                        ref, ref, ssem.at[p, 6 + n, 0], d3.at[p, n, i], row, col
                    ).wait_recv()

        last_tile = lref.at[pl.ds(T, T), pl.ds(T, T)]

        def last_send():
            return put(last_tile, last_tile, ssem.at[p, 8, 5], tsem.at[p], other, col)

        def r_place(q):
            return (x, y) if q == 0 else (y, x)

        def r_col(q, ma, mi):
            return 4 * ma + mi if q == 0 else 4 * mi + ma

        def r_scatter(i):
            to = jnp.where(h == 0, i, 4 * lax.rem(i, 4) + lax.div(i, 4))
            return put(
                m_ref.at[rows(i, 64), :], R.at[h, rows(i, 64), mycols],
                ssem.at[p, 13, i], r1.at[p, h, half], 2 * z + 1, to,
            )

        def r_own(fn):
            @pl.loop(0, 16)
            def _(i):
                @pl.when((h == 0) | (i != 4 * y + x))
                def _():
                    fn(i)

        def r_piece(q, ma, mi):
            return R.at[q, rows(4 * ma + mi, 64), :]

        def r_minor(q, t):
            ma, mi = r_place(q)
            ref = r_piece(q, ma, mi)
            return put(
                ref, ref, ssem.at[p, 16 + q, t - 1], r2.at[p, q, t - 1],
                row, r_col(q, ma, lax.rem(mi + t, 4)),
            )

        def r_minor_in(q, t):
            ma, mi = r_place(q)
            ref = r_piece(q, ma, lax.rem(mi + 4 - t, 4))
            put(ref, ref, ssem.at[p, 16, 0], r2.at[p, q, t - 1], row, col).wait_recv()

        def r_major(q, slot, t):
            ma, mi = r_place(q)
            ref = r_piece(q, ma, lax.rem(mi + 4 - slot, 4))
            return put(
                ref, ref, ssem.at[p, 16 + q, 3 + 3 * slot + t - 1], r3.at[p, q, 3 * slot + t - 1],
                row, r_col(q, lax.rem(ma + t, 4), mi),
            )

        def r_major_in(q, t):
            ma, mi = r_place(q)
            for slot in range(4):
                ref = r_piece(q, lax.rem(ma + 4 - t, 4), lax.rem(mi + 4 - slot, 4))
                put(
                    ref, ref, ssem.at[p, 16, 0], r3.at[p, q, 3 * slot + t - 1], row, col
                ).wait_recv()

        def r_core(t):
            ref = R.at[0, rows(lax.rem(x + 4 - t, 4), 256), :]
            return put(ref, ref, ssem.at[p, 18, t], r4.at[p, t], 2 * z, col)

        def r_first():
            for q in range(2):
                for s in range(2):
                    there = put(
                        m_ref.at[rows(0, 64), :], R.at[q, rows(0, 64), scols[s]],
                        ssem.at[p, 13, 0], r1.at[p, q, s], row, col,
                    )
                    if q == 0:
                        there.wait_recv()
                    else:
                        pl.when(jnp.logical_not((x == 0) & (y == first + s)))(there.wait_recv)
                for t in (1, 3, 2):
                    r_minor(q, t).start()
                for t in (1, 3, 2):
                    r_major(q, 0, t).start()

        def r_second():
            for slot in (1, 3, 2):
                for q in range(2):
                    r_minor_in(q, slot)
                    for t in (1, 3, 2):
                        r_major(q, slot, t).start()

        def c_rows(hh, q):
            return pl.ds(pl.multiple_of(hh * T + q * B, B), B)

        def c_tile(hh):
            return C.at[pl.ds(pl.multiple_of(hh * T, T), T), :]

        def c_first(t, which):
            zt = lax.rem(z + t, 4)
            q = zt if which == 0 else z
            return put(
                m_ref.at[rows(q, B), :], C.at[c_rows(h, q), :],
                ssem.at[p, 15, 2 * (t - 1) + which], c1.at[p, h, which], 2 * zt + 1, col,
            )

        def c_first_in(hh, which):
            ref = C.at[c_rows(hh, z if which == 0 else p), :]
            put(ref, ref, ssem.at[p, 15, 0], c1.at[p, hh, which], row, col).wait_recv()

        def c_second(hh, t):
            ref = C.at[c_rows(hh, z), :]
            return put(
                ref, ref, ssem.at[p, 14, 3 * hh + t - 1], c2.at[p, hh, t - 1],
                2 * lax.rem(z + t, 4) + 1, col,
            )

        def c_second_in(hh, t):
            ref = C.at[c_rows(hh, lax.rem(z + 4 - t, 4)), :]
            put(ref, ref, ssem.at[p, 14, 0], c2.at[p, hh, t - 1], row, col).wait_recv()

        def c_sibling():
            return put(
                m_ref.at[pl.ds(0, T), :], c_tile(0), ssem.at[p, 8, 7], c0.at[p], other, col
            )

        def c_core():
            return put(C, C, ssem.at[p, 8, 6], c3.at[p], other, col)

        def c_start():
            @pl.when(z == p)
            def _():
                for t in (1, 3, 2):
                    for which in (0, 1):
                        c_first(t, which).start()

                @pl.when(h == 0)
                def _():
                    c_sibling().start()

                @pl.when(h == 1)
                def _():
                    own = pltpu.make_async_copy(
                        m_ref.at[pl.ds(0, T), :], c_tile(1), lsem.at[p, 1]
                    )
                    own.start()
                    own.wait()

        def c_forward():
            @pl.when(z != p)
            def _():
                for hh in range(2):
                    c_first_in(hh, 0)
                    for t in (1, 2, 3):
                        @pl.when(lax.rem(z + t, 4) != p)
                        def _():
                            c_second(hh, t).start()

        def c_cross():
            @pl.when(z != p)
            def _():
                for hh in range(2):
                    c_first_in(hh, 1)
                    for t in (1, 2, 3):
                        @pl.when(lax.rem(z + 4 - t, 4) != p)
                        def _():
                            c_second_in(hh, t)

            @pl.when(z == p)
            def _():
                c_sibling().wait_recv()

        def l_core(g):
            ref = LW.at[pl.ds(g * H, W - g * H), pl.ds(g * H, H)]
            return put(ref, ref, ssem.at[p, 8, 1 + g], l4.at[p, g], other, col)

        d_start(0)
        head_start()
        d_start(1)

        @pl.when(is_source)
        def _():
            r_own(lambda i: r_scatter(i).start())

            @pl.when(h == 1)
            def _():
                own = pltpu.make_async_copy(
                    m_ref.at[rows(4 * y + x, 64), :],
                    R.at[1, rows(4 * y + x, 64), mycols], lsem.at[p, 0],
                )
                own.start()
                own.wait()

        def close(g, w0, l10, w1):
            low = dot3(split(w1), split(dot3(split(l10), split(w0), NN)), NN)
            big = jnp.concatenate(
                [
                    jnp.concatenate([w0, jnp.zeros_like(w0)], 1),
                    jnp.concatenate([-low, w1], 1),
                ],
                0,
            )
            wh[g], wl[g] = split(big)
            return big

        right_of = col > second
        in_panel = (col == first) | (col == second)
        top_below = row > second
        top_band = (row == first) | (row == second)
        column_half = jnp.where(col == second, 1, 0)

        def absorb(g):
            ds = pl.ds(g * H, H)
            wh[g], wl[g] = split(LW[ds, ds])
            for j in range(g + 1, 4):
                js = pl.ds(j * H, H)
                lh[js, ds], ll[js, ds] = split(LW[js, ds])

        def block(i):
            return pl.ds(i * H, H)

        def u_value(kb, cs):
            ks, done = block(kb), pl.ds(0, kb * H)
            value = C[ks, cs]
            if kb:
                value = value - dot3(
                    (lh[ks, done], ll[ks, done]), (uh[done, cs], ul[done, cs]), NN
                )
            return value

        def u_step(kb, ready=False):
            for n in range(2):
                cs = block(n)
                value = C[block(kb), cs] if ready else u_value(kb, cs)
                uk = dot3((wh[kb], wl[kb]), split(value), NN)
                uh[block(kb), cs], ul[block(kb), cs] = split(uk)
                if not ready:
                    C[block(kb), cs] = uk

        def u_ahead():
            for n in range(2):
                C[block(3), block(n)] = u_value(3, block(n))

        def x_value(q, g, kb):
            rs, ks, done = rows(g, H), block(kb), pl.ds(0, kb * H)
            value = R[q, rs, ks]
            if kb:
                value = value - dot3(
                    (xh[rs, done], xl[rs, done]), (lh[ks, done], ll[ks, done])
                )
            return value

        def keep_x(g, kb, xk):
            @pl.when(((g >= 2) | top_below) & in_panel & (column_half == kb // 2))
            def _():
                m_ref[rows(g, H), pl.ds(kb % 2 * H, H)] = xk

        def x_group(q, g):
            rs = rows(g, H)
            for kb in range(3):
                xk = dot3(split(x_value(q, g, kb)), (wh[kb], wl[kb]))
                xh[rs, block(kb)], xl[rs, block(kb)] = split(xk)
                if q:
                    keep_x(g, kb, xk)
                else:
                    R[q, rs, block(kb)] = xk
            R[q, rs, block(3)] = x_value(q, g, 3)

        def x_last(g):
            rs = rows(g, H)
            xk = dot3(split(R[h, rs, block(3)]), (wh[3], wl[3]))
            xh[rs, block(3)], xl[rs, block(3)] = split(xk)
            keep_x(g, 3, xk)

        def update(g):
            @pl.when(((g >= 2) | top_below) & right_of)
            def _():
                rs = rows(g, H)
                for n in range(2):
                    cs = pl.ds(n * H, H)
                    m_ref[rs, cs] = m_ref[rs, cs] - dot3(
                        (xh[rs, :], xl[rs, :]), (uh[:, cs], ul[:, cs]), NN
                    )

        def both(kb):
            u_step(kb)
            x_step(major, kb)

        def drain_source():
            for n in range(2):
                @pl.when(d_source(n))
                def _():
                    @pl.loop(0, parts[n][3])
                    def _(i):
                        d_scatter(n, i, mycols).wait_send()

            @pl.when(root)
            def _():
                @pl.loop(1, 16)
                def _(t):
                    h_plane(t).wait_send()

            @pl.when(is_source)
            def _():
                r_own(lambda i: r_scatter(i).wait_send())

            @pl.when(z == p)
            def _():
                for t in (1, 2, 3):
                    for which in (0, 1):
                        c_first(t, which).wait_send()

                @pl.when(h == 0)
                def _():
                    c_sibling().wait_send()

        def drain_r():
            for q in range(2):
                for t in (1, 2, 3):
                    r_minor(q, t).wait_send()
                    for slot in range(4):
                        r_major(q, slot, t).wait_send()

        def drain_c():
            @pl.when(z != p)
            def _():
                for t in (1, 2, 3):
                    @pl.when(lax.rem(z + t, 4) != p)
                    def _():
                        for hh in range(2):
                            c_second(hh, t).wait_send()

        @pl.when(h == 0)
        def _():
            head_wait()
            d_forward(0)
            d_forward(1)
            c_start()
            work[0:B, 0:B] = D[0:B, 0:B]

            def keep(rs, cs, value):
                lref[rs, cs] = value
                LW[rs, cs] = value
                pair_ = split(value)
                lh[rs, cs], ll[rs, cs] = pair_
                return pair_

            def close_root(g):
                s0, s1 = slice(g * H, g * H + B), slice(g * H + B, g * H + H)
                big = close(g, wref[s0, :], lref[s1, s0], wref[s1, :])
                LW[g * H : g * H + H, g * H : g * H + H] = big
                return wh[g], wl[g]

            def send(g):
                l_core(g).start()

            @pl.loop(0, W // B)
            def _(k):
                q0, q1, q2, q3 = (slice(i * H, i * H + H) for i in range(4))

                @pl.when(k == 1)
                def _():
                    e_across()
                    d_gather(0)
                    work[B:H, 0:H] = D[B:H, 0:H]

                @pl.when(k == 2)
                def _():
                    w = close_root(0)
                    xs = keep(q1, q0, dot3(split(D[q1, q0]), w))
                    work[q1, q1] = D[q1, q1] - dot3(xs, xs)

                @pl.when(k == 4)
                def _():
                    w = close_root(1)
                    e_gather()
                    es = keep(slice(T, W), q0, dot3(split(D[T:W, q0]), (wh[0], wl[0])))
                    send(0)
                    rest = D[T:W, q1] - dot3(es, (lh[q1, q0], ll[q1, q0]))
                    keep(slice(T, W), q1, dot3(split(rest), w))
                    send(1)
                    left = lambda r: (lh[r, 0:T], ll[r, 0:T])
                    work[q2, q2] = D[q2, q2] - dot3(left(q2), left(q2))
                    work[q3, q2] = D[q3, q2] - dot3(left(q3), left(q2))
                    work[q3, q3] = D[q3, q3] - dot3(left(q3), left(q3))

                @pl.when(k == 6)
                def _():
                    w = close_root(2)
                    xs = keep(q3, q2, dot3(split(work[q3, q2]), w))
                    send(2)
                    work[q3, q3] = work[q3, q3] - dot3(xs, xs)

                o = pl.multiple_of(k * B, B)
                here = pl.ds(o, B)
                before = pl.ds(pl.multiple_of(jnp.maximum(o - B, 0), B), B)

                @pl.when(lax.rem(k, 2) == 1)
                def _():
                    xk = dot3(split(work[here, before]), split(wref[before, :]))
                    lref[here, before] = xk
                    xs = split(xk)
                    work[here, here] = work[here, here] - dot3(xs, xs)

                upper, inverse = chol_block(work[here, here])
                wref[here, :] = inverse
                ri = lax.broadcasted_iota(jnp.int32, (B, B), 0)
                ci = lax.broadcasted_iota(jnp.int32, (B, B), 1)
                lref[here, here] = jnp.where(ri >= ci, upper.T, 0.0)

            close_root(3)
            l_core(3).start()

            @pl.when((row == first) & (col == second))
            def _():
                last_send().start()

            drain_source()
            c_core().wait_recv()
            for kb in range(3):
                uh[block(kb), :], ul[block(kb), :] = split(C[block(kb), :])
            for t in range(4):
                r_core(t).wait_recv()

            @pl.loop(0, 4)
            def _(g):
                rs = rows(g, H)
                for kb in range(3):
                    xk = R[0, rs, block(kb)]
                    xh[rs, block(kb)], xl[rs, block(kb)] = split(xk)
                    keep_x(g, kb, xk)

        @pl.when(h == 1)
        def _():
            r_first()
            c_start()
            c_forward()
            r_second()
            c_cross()
            drain_source()
            drain_c()
            for kb in range(3):
                l_core(kb).wait_recv()
                absorb(kb)
                u_step(kb)
            u_ahead()
            c_core().start()
            for q in range(2):
                for t in (1, 3, 2):
                    r_major_in(q, t)
            drain_r()

            @pl.loop(0, 4)
            def _(t):
                g = lax.rem(x + 4 - t, 4)
                x_group(0, g)
                r_core(t).start()

            @pl.loop(0, 4)
            def _(g):
                x_group(1, g)

            l_core(3).wait_recv()
            absorb(3)

        u_step(3, True)

        @pl.loop(0, 4)
        def _(g):
            x_last(g)
            update(g)

        @pl.when(top_band & right_of)
        def _():
            m_ref[0:T, :] = jnp.zeros((T, T), jnp.float32)

        @pl.when(top_band & in_panel)
        def _():
            @pl.when(root)
            def _():
                m_ref[0:T, :] = lref[0:T, 0:T]

            @pl.when((row == first) & (col == second))
            def _():
                m_ref[0:T, :] = jnp.zeros((T, T), jnp.float32)

            @pl.when((row == second) & (col == first))
            def _():
                m_ref[0:T, :] = LW[T:W, 0:T]

            @pl.when((row == second) & (col == second))
            def _():
                last_send().wait_recv()
                m_ref[0:T, :] = last_tile[...]

        @pl.when(h == 1)
        def _():
            for t in range(4):
                r_core(t).wait_send()

        @pl.when(h == 1)
        def _():
            c_core().wait_send()

        for n in range(2):
            @pl.when(d_owner(n))
            def _():
                @pl.when(z == p)
                def _():
                    for t in (1, 2, 3):
                        d_planes(n, t).wait_send()

                if n == 0:
                    @pl.loop(1, 16)
                    def _(t):
                        d_spread(n, t).wait_send()
                else:
                    for t in (1, 3, 2):
                        e_row(t).wait_send()

        @pl.when(h == 0)
        def _():
            for t in (1, 3, 2):
                e_column(t).wait_send()
            for g in range(4):
                l_core(g).wait_send()

            @pl.when(z == p)
            def _():
                for t in (1, 2, 3):
                    h_planes(t).wait_send()

            @pl.when((row == first) & (col == second))
            def _():
                last_send().wait_send()

    pl.loop(0, 2)(panel)


def local(kernel):
    f32, b16 = jnp.float32, jnp.bfloat16
    dma = pltpu.SemaphoreType.DMA
    return pl.pallas_call(
        body,
        out_shape=jax.ShapeDtypeStruct((W, T), f32),
        in_specs=[pl.BlockSpec(memory_space=pl.ANY)],
        out_specs=pl.BlockSpec(memory_space=pltpu.VMEM),
        scratch_shapes=[
            pltpu.VMEM((2, 2, W, W), f32),
            pltpu.VMEM((2, W, T), f32),
            pltpu.VMEM((2, W, W), f32),
            pltpu.VMEM((2, W, W), f32),
            pltpu.VMEM((W, W), f32),
            pltpu.VMEM((W, W), f32),
            pltpu.VMEM((W, B), f32),
            pltpu.VMEM((W, W), b16),
            pltpu.VMEM((W, W), b16),
            pltpu.VMEM((4, H, H), b16),
            pltpu.VMEM((4, H, H), b16),
            pltpu.VMEM((W, W), b16),
            pltpu.VMEM((W, W), b16),
            pltpu.VMEM((W, T), b16),
            pltpu.VMEM((W, T), b16),
            dma((2, 19, 16)),
            dma((2, 2, 2)), dma((2, 2, 3)), dma((2, 2, 12)), dma((2, 4)),
            dma((2,)), dma((2, 2, 2)), dma((2, 2, 3)), dma((2,)),
            dma((2, 3)), dma((2, 2)), dma((2, 2, 12)), dma((2, 2)),
            dma((2, 4)),
            dma((2,)),
            dma((2, 3)),
        ],
        compiler_params=pltpu.CompilerParams(
            collective_id=0, has_side_effects=True, vmem_limit_bytes=62 * 1024 * 1024
        ),
        cost_estimate=pl.CostEstimate(
            flops=20_000_000_000, bytes_accessed=8_000_000, transcendentals=0
        ),
        name="two_panels",
    )(kernel)


def solution(mesh):
    return jax.shard_map(
        local,
        mesh=mesh,
        in_specs=(P("row", "col"),),
        out_specs=P("row", "col"),
        check_vma=False,
    )
```

```python
import functools

import jax
import jax.numpy as jnp
from jax import lax
from jax.experimental import pallas as pl
from jax.experimental.pallas import tpu as pltpu
from jax.sharding import PartitionSpec as P

T = 512
W = 1024
B = 128
H = 256
MESH = pl.DeviceIdType.MESH
NT = (((1,), (1,)), ((), ()))
NN = (((1,), (0,)), ((), ()))


def split(x):
    hi = x.astype(jnp.bfloat16)
    lo = (x - hi.astype(jnp.float32)).astype(jnp.bfloat16)
    return hi, lo


def dot3(a, b, dims=NT):
    (ah, al), (bh, bl) = a, b
    d = functools.partial(
        lax.dot_general, dimension_numbers=dims, preferred_element_type=jnp.float32
    )
    return d(ah, bh) + (d(ah, bl) + d(al, bh))


def lane(x, i):
    return jnp.broadcast_to(x[:, i : i + 1], (8, B))


def sub(x, i):
    return jnp.broadcast_to(x[i : i + 1, :], (8, B))


def chol_block(block):
    n = B // 8
    li = lax.broadcasted_iota(jnp.int32, (8, B), 1)
    si = lax.broadcasted_iota(jnp.int32, (8, B), 0)
    rows = [block[8 * i : 8 * i + 8] for i in range(n)]
    eye = [(li == si + 8 * i).astype(jnp.float32) for i in range(n)]
    upper, inverse = [], []

    def merge(xs):
        out = xs[0]
        for t in range(1, 8):
            out = jnp.where(si == t, xs[t], out)
        return out

    for j in range(n):
        o = 8 * j
        cols = [lane(rows[j], o + q) for q in range(8)]
        m = {(p, q): sub(cols[q], p) for q in range(8) for p in range(q, 8)}
        rb = [sub(rows[j], p) for p in range(8)]
        eb = [sub(eye[j], p) for p in range(8)]
        nxt = j + 1 < n
        if nxt:
            raw = [[lane(rows[i], o + q) for q in range(8)] for i in range(j + 1, n)]
            nc = list(raw[0])
        rk = [None] * 8
        fs = {}
        for k in range(8):
            rk[k] = 1.0 / m[k, k]
            for q in range(k + 1, 8):
                if q == k + 1:
                    m[q, q] = m[q, q] - (m[q, k] * m[q, k]) * rk[k]
                f = m[q, k] * rk[k]
                fs[q, k] = f
                for p in range(q + (1 if q == k + 1 else 0), 8):
                    m[p, q] = m[p, q] - m[p, k] * f
                rb[q] = rb[q] - f * rb[k]
                eb[q] = eb[q] - f * eb[k]
                if nxt:
                    nc[q] = nc[q] - f * nc[k]
            if nxt:
                c = nc[k] * rk[k]
                rows[j + 1] = rows[j + 1] - c * rb[k]
                eye[j + 1] = eye[j + 1] - c * eb[k]
        sk = lax.rsqrt(merge([m[k, k] for k in range(8)]))
        upper.append(merge(rb) * sk)
        inverse.append(merge(eb) * sk)
        if j + 2 < n:
            vr = [rb[k] * rk[k] for k in range(8)]
            ve = [eb[k] * rk[k] for k in range(8)]
            for q in range(7, -1, -1):
                for k in range(q):
                    vr[k] = vr[k] - fs[q, k] * vr[q]
                    ve[k] = ve[k] - fs[q, k] * ve[q]
            for i in range(j + 2, n):
                ar, ae = rows[i], eye[i]
                for q in range(8):
                    c = raw[i - j - 1][q]
                    ar = ar - c * vr[q]
                    ae = ae - c * ve[q]
                rows[i], eye[i] = ar, ae
    return jnp.concatenate(upper, 0), jnp.concatenate(inverse, 0)


def body(
    a_ref, m_ref, rbuf, cbuf, lw, dbuf, work, lref, wref, lh, ll, wh, wl, xh, xl, uh, ul,
    ssem, r1, r2, r3, r4, c0, c1, c2, c3, d1, d2, d3, d5, l4, tsem, lsem,
):
    row = lax.axis_index("row")
    col = lax.axis_index("col")
    h = lax.rem(row, 2)
    z = lax.div(row, 2)
    x = lax.div(col, 4)
    y = lax.rem(col, 4)
    major = jnp.where(h == 0, x, y)
    def put(src, dst, send, recv, row_to, col_to):
        return pltpu.make_async_remote_copy(
            src_ref=src, dst_ref=dst, send_sem=send, recv_sem=recv,
            device_id=(row_to, col_to), device_id_type=MESH,
        )

    def rows(start, size):
        return pl.ds(pl.multiple_of(start * size, size), size)

    barrier = pltpu.get_barrier_semaphore()

    def greet(row_to, col_to):
        pl.semaphore_signal(barrier, inc=1, device_id=(row_to, col_to), device_id_type=MESH)

    @pl.loop(1, 16)
    def _(t):
        greet(row, lax.rem(col + t, 16))
        greet(2 * z + 1 - h, lax.rem(col + t, 16))

    for t in range(1, 4):
        greet(2 * lax.rem(z + t, 4), col)
        greet(2 * lax.rem(z + t, 4) + 1, col)
    greet(2 * z + 1 - h, col)

    @pl.when((h == 0) & (x == 0))
    def _():
        @pl.loop(0, 32)
        def _(i):
            @pl.when((lax.div(i, 4) != row) | (lax.rem(i, 4) != col))
            def _():
                greet(lax.div(i, 4), lax.rem(i, 4))

    load = pltpu.make_async_copy(a_ref, m_ref, lsem.at[0, 2])
    load.start()

    @pl.when(h == 0)
    def _():
        lref[...] = jnp.zeros_like(lref)

    load.wait()
    @pl.when(x != 0)
    def _():
        pl.semaphore_wait(barrier, 37)

    @pl.when((x == 0) & (h == 0))
    def _():
        pl.semaphore_wait(barrier, 52)

    @pl.when((x == 0) & (h == 1))
    def _():
        pl.semaphore_wait(barrier, 53)

    def panel(p):
        first = 2 * p
        second = first + 1
        is_source = (x == 0) & ((y == first) | (y == second))
        root = (row == first) & (col == first)
        half = jnp.where(y == second, 1, 0)
        mycols = pl.ds(pl.multiple_of(half * T, T), T)
        scols = [pl.ds(0, T), pl.ds(T, T)]
        R, C, LW, D = rbuf.at[p], cbuf.at[p], lw.at[p], dbuf.at[p]
        other = 2 * z + 1 - h

        head = D.at[pl.ds(0, B), pl.ds(0, B)]
        parts = ((B, 24, T), (T, 32, W))

        def h_plane(t):
            return put(
                m_ref.at[pl.ds(0, B), pl.ds(0, B)], head, ssem.at[p, 5, t], d5.at[p, 0],
                row, lax.rem(col + t, 16),
            )

        def h_planes(t):
            return put(
                head, head, ssem.at[p, 2, t], d5.at[p, 1], 2 * lax.rem(z + t, 4) + h, col
            )

        def head_start():
            @pl.when(root)
            def _():
                @pl.loop(1, 16)
                def _(t):
                    h_plane(t).start()

                own = pltpu.make_async_copy(
                    m_ref.at[pl.ds(0, B), pl.ds(0, B)], head, lsem.at[p, 2]
                )
                own.start()
                own.wait()
                for t in (1, 2, 3):
                    h_planes(t).start()

        def head_wait():
            @pl.when(z == p)
            def _():
                @pl.when(jnp.logical_not(root))
                def _():
                    h_plane(1).wait_recv()
                    for t in (1, 2, 3):
                        h_planes(t).start()

            @pl.when(z != p)
            def _():
                h_planes(1).wait_recv()

        def d_rows(n, i, count=1):
            start, size, width = parts[n]
            return D.at[
                pl.ds(pl.multiple_of(start + i * size, 8), count * size), pl.ds(0, width)
            ]

        def d_scatter(n, i, s):
            start, size, _w = parts[n]
            here = pl.ds(pl.multiple_of((0 if n else start) + i * size, 8), size)
            there = pl.ds(pl.multiple_of(start + i * size, 8), size)
            return (
                m_ref.at[here, :], D.at[there, s if n else pl.ds(0, T)],
                ssem.at[p, n, i], d1.at[p, n + (half if n else 0)],
                2 * lax.div(i, 4), lax.rem(i, 4),
            )

        def d_source(n):
            return is_source & (row == second) if n else root

        def d_out(n, fn):
            @pl.loop(0, 16)
            def _(i):
                if n:
                    fn(put(*d_scatter(n, i, mycols)))
                else:
                    @pl.when(i != d_mine)
                    def _():
                        fn(put(*d_scatter(n, i, mycols)))

        d_mine = 4 * z + y

        def d_start(n):
            @pl.when(d_source(n))
            def _():
                d_out(n, lambda c: c.start())
                if n == 0:
                    src, dst = d_scatter(n, d_mine, mycols)[:2]
                    own = pltpu.make_async_copy(src, dst, lsem.at[p, 3])
                    own.start()
                    own.wait()

        def d_x(n, t):
            ref = d_rows(n, d_mine)
            return put(
                ref, ref, ssem.at[p, 3 + n, t], d2.at[p, n], row, 4 * lax.rem(x + t, 4) + y
            )

        def d_y(n, t):
            ref = d_rows(n, d_mine)
            return put(
                ref, ref, ssem.at[p, 6 + n, t], d3.at[p, n, t], row, 4 * x + lax.rem(y + t, 4)
            )

        def d_z(n, t):
            ref = d_rows(n, 4 * z, 4)
            return put(
                ref, ref, ssem.at[p, 6 + n, 4 + t], d3.at[p, n, 4 + t],
                2 * lax.rem(z + t, 4) + h, col,
            )

        def d_forward(n):
            @pl.when(x == 0)
            def _():
                for s in range(1 + n):
                    here = put(*d_scatter(n, d_mine, scols[s])[:3], d1.at[p, n + s], row, col)
                    if n:
                        here.wait_recv()
                    else:
                        pl.when(jnp.logical_not(root))(here.wait_recv)
                for t in (1, 3, 2):
                    d_x(n, t).start()

        def d_second(n):
            pl.when(x != 0)(d_x(n, 1).wait_recv)
            for t in (1, 3, 2):
                d_y(n, t).start()

        def d_third(n):
            for t in (1, 3, 2):
                ref = d_rows(n, 4 * z + lax.rem(y + 4 - t, 4))
                put(ref, ref, ssem.at[p, 6 + n, 0], d3.at[p, n, t], row, col).wait_recv()
            for t in (1, 3, 2):
                d_z(n, t).start()

        def d_gather(n):
            for t in (1, 3, 2):
                ref = d_rows(n, 4 * lax.rem(z + 4 - t, 4), 4)
                put(ref, ref, ssem.at[p, 6 + n, 0], d3.at[p, n, 4 + t], row, col).wait_recv()

        last_tile = lref.at[pl.ds(T, T), pl.ds(T, T)]

        def last_send():
            return put(last_tile, last_tile, ssem.at[p, 8, 5], tsem.at[p], other, col)

        def r_place(q):
            return (x, y) if q == 0 else (y, x)

        def r_col(q, ma, mi):
            return 4 * ma + mi if q == 0 else 4 * mi + ma

        def r_scatter(i):
            to = jnp.where(h == 0, i, 4 * lax.rem(i, 4) + lax.div(i, 4))
            return put(
                m_ref.at[rows(i, 64), :], R.at[h, rows(i, 64), mycols],
                ssem.at[p, 13, i], r1.at[p, h, half], 2 * z + 1, to,
            )

        def r_own(fn):
            @pl.loop(0, 16)
            def _(i):
                @pl.when((h == 0) | (i != 4 * y + x))
                def _():
                    fn(i)

        def r_piece(q, ma, mi):
            return R.at[q, rows(4 * ma + mi, 64), :]

        def r_minor(q, t):
            ma, mi = r_place(q)
            ref = r_piece(q, ma, mi)
            return put(
                ref, ref, ssem.at[p, 16 + q, t - 1], r2.at[p, q, t - 1],
                row, r_col(q, ma, lax.rem(mi + t, 4)),
            )

        def r_minor_in(q, t):
            ma, mi = r_place(q)
            ref = r_piece(q, ma, lax.rem(mi + 4 - t, 4))
            put(ref, ref, ssem.at[p, 16, 0], r2.at[p, q, t - 1], row, col).wait_recv()

        def r_major(q, slot, t):
            ma, mi = r_place(q)
            ref = r_piece(q, ma, lax.rem(mi + 4 - slot, 4))
            return put(
                ref, ref, ssem.at[p, 16 + q, 3 + 3 * slot + t - 1], r3.at[p, q, 3 * slot + t - 1],
                row, r_col(q, lax.rem(ma + t, 4), mi),
            )

        def r_major_in(q, t):
            ma, mi = r_place(q)
            for slot in range(4):
                ref = r_piece(q, lax.rem(ma + 4 - t, 4), lax.rem(mi + 4 - slot, 4))
                put(
                    ref, ref, ssem.at[p, 16, 0], r3.at[p, q, 3 * slot + t - 1], row, col
                ).wait_recv()

        def r_core(t):
            ref = R.at[0, rows(lax.rem(x + 4 - t, 4), 256), :]
            return put(ref, ref, ssem.at[p, 18, t], r4.at[p, t], 2 * z, col)

        def r_first():
            for q in range(2):
                for s in range(2):
                    there = put(
                        m_ref.at[rows(0, 64), :], R.at[q, rows(0, 64), scols[s]],
                        ssem.at[p, 13, 0], r1.at[p, q, s], row, col,
                    )
                    if q == 0:
                        there.wait_recv()
                    else:
                        pl.when(jnp.logical_not((x == 0) & (y == first + s)))(there.wait_recv)
                for t in (1, 3, 2):
                    r_minor(q, t).start()
                for t in (1, 3, 2):
                    r_major(q, 0, t).start()

        def r_second():
            for slot in (1, 3, 2):
                for q in range(2):
                    r_minor_in(q, slot)
                    for t in (1, 3, 2):
                        r_major(q, slot, t).start()

        def c_rows(hh, q):
            return pl.ds(pl.multiple_of(hh * T + q * B, B), B)

        def c_tile(hh):
            return C.at[pl.ds(pl.multiple_of(hh * T, T), T), :]

        def c_first(hh, t, which):
            zt = lax.rem(z + t, 4)
            ref = C.at[c_rows(hh, zt if which == 0 else z), :]
            return put(
                ref, ref, ssem.at[p, 15, 6 * hh + 2 * (t - 1) + which], c1.at[p, hh, which],
                2 * zt + 1, col,
            )

        def c_first_in(hh, which):
            ref = C.at[c_rows(hh, z if which == 0 else p), :]
            put(ref, ref, ssem.at[p, 15, 0], c1.at[p, hh, which], row, col).wait_recv()

        def c_second(hh, t):
            ref = C.at[c_rows(hh, z), :]
            return put(
                ref, ref, ssem.at[p, 14, 3 * hh + t - 1], c2.at[p, hh, t - 1],
                2 * lax.rem(z + t, 4) + 1, col,
            )

        def c_second_in(hh, t):
            ref = C.at[c_rows(hh, lax.rem(z + 4 - t, 4)), :]
            put(ref, ref, ssem.at[p, 14, 0], c2.at[p, hh, t - 1], row, col).wait_recv()

        def c_sibling():
            return put(
                m_ref.at[pl.ds(0, T), :], c_tile(0), ssem.at[p, 8, 7], c0.at[p], other, col
            )

        def c_core():
            return put(C, C, ssem.at[p, 8, 6], c3.at[p], other, col)

        def c_start():
            @pl.when((z == p) & (h == 1))
            def _():
                own = pltpu.make_async_copy(
                    m_ref.at[pl.ds(0, T), :], c_tile(1), lsem.at[p, 1]
                )
                own.start()
                own.wait()
                for hh in (1, 0):
                    if hh == 0:
                        c_sibling().wait_recv()
                    for t in (1, 3, 2):
                        for which in (0, 1):
                            c_first(hh, t, which).start()

        def c_forward():
            @pl.when(z != p)
            def _():
                for hh in range(2):
                    c_first_in(hh, 0)
                    for t in (1, 2, 3):
                        @pl.when(lax.rem(z + t, 4) != p)
                        def _():
                            c_second(hh, t).start()

        def c_cross():
            @pl.when(z != p)
            def _():
                for hh in range(2):
                    c_first_in(hh, 1)
                    for t in (1, 2, 3):
                        @pl.when(lax.rem(z + 4 - t, 4) != p)
                        def _():
                            c_second_in(hh, t)

        def l_core(g):
            ref = LW.at[pl.ds(g * H, W - g * H), pl.ds(g * H, H)]
            return put(ref, ref, ssem.at[p, 8, 1 + g], l4.at[p, g], other, col)

        d_start(0)
        head_start()
        d_start(1)

        @pl.when((z == p) & (h == 0))
        def _():
            c_sibling().start()

        @pl.when(is_source)
        def _():
            r_own(lambda i: r_scatter(i).start())

            @pl.when(h == 1)
            def _():
                own = pltpu.make_async_copy(
                    m_ref.at[rows(4 * y + x, 64), :],
                    R.at[1, rows(4 * y + x, 64), mycols], lsem.at[p, 0],
                )
                own.start()
                own.wait()

        def close(g, w0, l10, w1):
            low = dot3(split(w1), split(dot3(split(l10), split(w0), NN)), NN)
            big = jnp.concatenate(
                [
                    jnp.concatenate([w0, jnp.zeros_like(w0)], 1),
                    jnp.concatenate([-low, w1], 1),
                ],
                0,
            )
            wh[g], wl[g] = split(big)
            return big

        right_of = col > second
        in_panel = (col == first) | (col == second)
        top_below = row > second
        top_band = (row == first) | (row == second)
        column_half = jnp.where(col == second, 1, 0)

        def absorb(g):
            ds = pl.ds(g * H, H)
            wh[g], wl[g] = split(LW[ds, ds])
            for j in range(g + 1, 4):
                js = pl.ds(j * H, H)
                lh[js, ds], ll[js, ds] = split(LW[js, ds])

        def block(i):
            return pl.ds(i * H, H)

        def u_value(kb, cs):
            ks, done = block(kb), pl.ds(0, kb * H)
            value = C[ks, cs]
            if kb:
                value = value - dot3(
                    (lh[ks, done], ll[ks, done]), (uh[done, cs], ul[done, cs]), NN
                )
            return value

        def u_step(kb, ready=False):
            for n in range(2):
                cs = block(n)
                value = C[block(kb), cs] if ready else u_value(kb, cs)
                uk = dot3((wh[kb], wl[kb]), split(value), NN)
                uh[block(kb), cs], ul[block(kb), cs] = split(uk)
                if not ready:
                    C[block(kb), cs] = uk

        def u_ahead():
            for n in range(2):
                C[block(3), block(n)] = u_value(3, block(n))

        def x_value(q, g, kb):
            rs, ks, done = rows(g, H), block(kb), pl.ds(0, kb * H)
            value = R[q, rs, ks]
            if kb:
                value = value - dot3(
                    (xh[rs, done], xl[rs, done]), (lh[ks, done], ll[ks, done])
                )
            return value

        def keep_x(g, kb, xk):
            @pl.when(((g >= 2) | top_below) & in_panel & (column_half == kb // 2))
            def _():
                m_ref[rows(g, H), pl.ds(kb % 2 * H, H)] = xk

        def x_group(q, g):
            rs = rows(g, H)
            for kb in range(3):
                xk = dot3(split(x_value(q, g, kb)), (wh[kb], wl[kb]))
                xh[rs, block(kb)], xl[rs, block(kb)] = split(xk)
                if q:
                    keep_x(g, kb, xk)
                else:
                    R[q, rs, block(kb)] = xk
            R[q, rs, block(3)] = x_value(q, g, 3)

        def x_last(g):
            rs = rows(g, H)
            xk = dot3(split(R[h, rs, block(3)]), (wh[3], wl[3]))
            xh[rs, block(3)], xl[rs, block(3)] = split(xk)
            keep_x(g, 3, xk)

        def update(g):
            @pl.when(((g >= 2) | top_below) & right_of)
            def _():
                rs = rows(g, H)
                for n in range(2):
                    cs = pl.ds(n * H, H)
                    m_ref[rs, cs] = m_ref[rs, cs] - dot3(
                        (xh[rs, :], xl[rs, :]), (uh[:, cs], ul[:, cs]), NN
                    )

        def both(kb):
            u_step(kb)
            x_step(major, kb)

        def drain_source():
            for n in range(2):
                @pl.when(d_source(n))
                def _():
                    d_out(n, lambda c: c.wait_send())

            @pl.when(root)
            def _():
                @pl.loop(1, 16)
                def _(t):
                    h_plane(t).wait_send()

            @pl.when(is_source)
            def _():
                r_own(lambda i: r_scatter(i).wait_send())

            @pl.when((z == p) & (h == 1))
            def _():
                for hh in range(2):
                    for t in (1, 2, 3):
                        for which in (0, 1):
                            c_first(hh, t, which).wait_send()

            @pl.when((z == p) & (h == 0))
            def _():
                c_sibling().wait_send()

        def drain_r():
            for q in range(2):
                for t in (1, 2, 3):
                    r_minor(q, t).wait_send()
                    for slot in range(4):
                        r_major(q, slot, t).wait_send()

        def drain_c():
            @pl.when(z != p)
            def _():
                for t in (1, 2, 3):
                    @pl.when(lax.rem(z + t, 4) != p)
                    def _():
                        for hh in range(2):
                            c_second(hh, t).wait_send()

        @pl.when(h == 0)
        def _():
            head_wait()
            d_forward(0)
            d_forward(1)
            d_second(0)
            d_third(0)
            d_second(1)
            work[0:B, 0:B] = D[0:B, 0:B]

            def keep(rs, cs, value):
                lref[rs, cs] = value
                LW[rs, cs] = value
                pair_ = split(value)
                lh[rs, cs], ll[rs, cs] = pair_
                return pair_

            def close_root(g):
                s0, s1 = slice(g * H, g * H + B), slice(g * H + B, g * H + H)
                big = close(g, wref[s0, :], lref[s1, s0], wref[s1, :])
                LW[g * H : g * H + H, g * H : g * H + H] = big
                return wh[g], wl[g]

            def send(g):
                l_core(g).start()

            @pl.loop(0, W // B)
            def _(k):
                q0, q1, q2, q3 = (slice(i * H, i * H + H) for i in range(4))

                @pl.when(k == 1)
                def _():
                    d_third(1)
                    d_gather(0)
                    work[B:H, 0:H] = D[B:H, 0:H]

                @pl.when(k == 2)
                def _():
                    w = close_root(0)
                    xs = keep(q1, q0, dot3(split(D[q1, q0]), w))
                    work[q1, q1] = D[q1, q1] - dot3(xs, xs)

                @pl.when(k == 4)
                def _():
                    w = close_root(1)
                    d_gather(1)
                    es = keep(slice(T, W), q0, dot3(split(D[T:W, q0]), (wh[0], wl[0])))
                    send(0)
                    rest = D[T:W, q1] - dot3(es, (lh[q1, q0], ll[q1, q0]))
                    keep(slice(T, W), q1, dot3(split(rest), w))
                    send(1)
                    left = lambda r: (lh[r, 0:T], ll[r, 0:T])
                    work[q2, q2] = D[q2, q2] - dot3(left(q2), left(q2))
                    work[q3, q2] = D[q3, q2] - dot3(left(q3), left(q2))
                    work[q3, q3] = D[q3, q3] - dot3(left(q3), left(q3))

                @pl.when(k == 6)
                def _():
                    w = close_root(2)
                    xs = keep(q3, q2, dot3(split(work[q3, q2]), w))
                    send(2)
                    work[q3, q3] = work[q3, q3] - dot3(xs, xs)

                o = pl.multiple_of(k * B, B)
                here = pl.ds(o, B)
                before = pl.ds(pl.multiple_of(jnp.maximum(o - B, 0), B), B)

                @pl.when(lax.rem(k, 2) == 1)
                def _():
                    xk = dot3(split(work[here, before]), split(wref[before, :]))
                    lref[here, before] = xk
                    xs = split(xk)
                    work[here, here] = work[here, here] - dot3(xs, xs)

                upper, inverse = chol_block(work[here, here])
                wref[here, :] = inverse
                ri = lax.broadcasted_iota(jnp.int32, (B, B), 0)
                ci = lax.broadcasted_iota(jnp.int32, (B, B), 1)
                lref[here, here] = jnp.where(ri >= ci, upper.T, 0.0)

            close_root(3)
            l_core(3).start()

            @pl.when((row == first) & (col == second))
            def _():
                last_send().start()

            drain_source()
            c_core().wait_recv()
            for kb in range(3):
                uh[block(kb), :], ul[block(kb), :] = split(C[block(kb), :])
            for t in range(4):
                r_core(t).wait_recv()

            @pl.loop(0, 4)
            def _(g):
                rs = rows(g, H)
                for kb in range(3):
                    xk = R[0, rs, block(kb)]
                    xh[rs, block(kb)], xl[rs, block(kb)] = split(xk)
                    keep_x(g, kb, xk)

        @pl.when(h == 1)
        def _():
            c_start()
            r_first()
            c_forward()
            r_second()
            c_cross()
            drain_source()
            drain_c()
            for kb in range(3):
                l_core(kb).wait_recv()
                absorb(kb)
                u_step(kb)
            u_ahead()
            c_core().start()
            for q in range(2):
                for t in (1, 3, 2):
                    r_major_in(q, t)
            drain_r()

            @pl.loop(0, 4)
            def _(t):
                g = lax.rem(x + 4 - t, 4)
                x_group(0, g)
                r_core(t).start()

            @pl.loop(0, 4)
            def _(g):
                x_group(1, g)

            l_core(3).wait_recv()
            absorb(3)

        u_step(3, True)

        @pl.loop(0, 4)
        def _(g):
            x_last(g)
            update(g)

        @pl.when(top_band & right_of)
        def _():
            m_ref[0:T, :] = jnp.zeros((T, T), jnp.float32)

        @pl.when(top_band & in_panel)
        def _():
            @pl.when(root)
            def _():
                m_ref[0:T, :] = lref[0:T, 0:T]

            @pl.when((row == first) & (col == second))
            def _():
                m_ref[0:T, :] = jnp.zeros((T, T), jnp.float32)

            @pl.when((row == second) & (col == first))
            def _():
                m_ref[0:T, :] = LW[T:W, 0:T]

            @pl.when((row == second) & (col == second))
            def _():
                last_send().wait_recv()
                m_ref[0:T, :] = last_tile[...]

        @pl.when(h == 1)
        def _():
            for t in range(4):
                r_core(t).wait_send()

        @pl.when(h == 1)
        def _():
            c_core().wait_send()

        @pl.when(h == 0)
        def _():
            for n in range(2):
                for t in (1, 3, 2):
                    d_y(n, t).wait_send()
                    d_z(n, t).wait_send()

                @pl.when(x == 0)
                def _():
                    for t in (1, 3, 2):
                        d_x(n, t).wait_send()

            for g in range(4):
                l_core(g).wait_send()

            @pl.when(z == p)
            def _():
                for t in (1, 2, 3):
                    h_planes(t).wait_send()

            @pl.when((row == first) & (col == second))
            def _():
                last_send().wait_send()

    pl.loop(0, 2)(panel)


def local(kernel):
    f32, b16 = jnp.float32, jnp.bfloat16
    dma = pltpu.SemaphoreType.DMA
    return pl.pallas_call(
        body,
        out_shape=jax.ShapeDtypeStruct((W, T), f32),
        in_specs=[pl.BlockSpec(memory_space=pl.ANY)],
        out_specs=pl.BlockSpec(memory_space=pltpu.VMEM),
        scratch_shapes=[
            pltpu.VMEM((2, 2, W, W), f32),
            pltpu.VMEM((2, W, T), f32),
            pltpu.VMEM((2, W, W), f32),
            pltpu.VMEM((2, W, W), f32),
            pltpu.VMEM((W, W), f32),
            pltpu.VMEM((W, W), f32),
            pltpu.VMEM((W, B), f32),
            pltpu.VMEM((W, W), b16),
            pltpu.VMEM((W, W), b16),
            pltpu.VMEM((4, H, H), b16),
            pltpu.VMEM((4, H, H), b16),
            pltpu.VMEM((W, W), b16),
            pltpu.VMEM((W, W), b16),
            pltpu.VMEM((W, T), b16),
            pltpu.VMEM((W, T), b16),
            dma((2, 19, 16)),
            dma((2, 2, 2)), dma((2, 2, 3)), dma((2, 2, 12)), dma((2, 4)),
            dma((2,)), dma((2, 2, 2)), dma((2, 2, 3)), dma((2,)),
            dma((2, 3)), dma((2, 2)), dma((2, 2, 12)), dma((2, 2)),
            dma((2, 4)),
            dma((2,)),
            dma((2, 4)),
        ],
        compiler_params=pltpu.CompilerParams(
            collective_id=0, has_side_effects=True, vmem_limit_bytes=62 * 1024 * 1024
        ),
        cost_estimate=pl.CostEstimate(
            flops=20_000_000_000, bytes_accessed=8_000_000, transcendentals=0
        ),
        name="two_panels",
    )(kernel)


def solution(mesh):
    return jax.shard_map(
        local,
        mesh=mesh,
        in_specs=(P("row", "col"),),
        out_specs=P("row", "col"),
        check_vma=False,
    )
```

```python
import functools

import jax
import jax.numpy as jnp
from jax import lax
from jax.experimental import pallas as pl
from jax.experimental.pallas import tpu as pltpu
from jax.sharding import PartitionSpec as P

T = 512
W = 1024
B = 128
H = 256
MESH = pl.DeviceIdType.MESH
NT = (((1,), (1,)), ((), ()))
NN = (((1,), (0,)), ((), ()))


def split(x):
    hi = x.astype(jnp.bfloat16)
    lo = (x - hi.astype(jnp.float32)).astype(jnp.bfloat16)
    return hi, lo


def dot3(a, b, dims=NT):
    (ah, al), (bh, bl) = a, b
    d = functools.partial(
        lax.dot_general, dimension_numbers=dims, preferred_element_type=jnp.float32
    )
    return d(ah, bh) + (d(ah, bl) + d(al, bh))


def lane(x, i):
    return jnp.broadcast_to(x[:, i : i + 1], (8, B))


def sub(x, i):
    return jnp.broadcast_to(x[i : i + 1, :], (8, B))


def chol_block(block):
    n = B // 8
    li = lax.broadcasted_iota(jnp.int32, (8, B), 1)
    si = lax.broadcasted_iota(jnp.int32, (8, B), 0)
    rows = [block[8 * i : 8 * i + 8] for i in range(n)]
    eye = [(li == si + 8 * i).astype(jnp.float32) for i in range(n)]
    upper, inverse = [], []

    def merge(xs):
        out = xs[0]
        for t in range(1, 8):
            out = jnp.where(si == t, xs[t], out)
        return out

    for j in range(n):
        o = 8 * j
        cols = [lane(rows[j], o + q) for q in range(8)]
        m = {(p, q): sub(cols[q], p) for q in range(8) for p in range(q, 8)}
        rb = [sub(rows[j], p) for p in range(8)]
        eb = [sub(eye[j], p) for p in range(8)]
        nxt = j + 1 < n
        if nxt:
            raw = [[lane(rows[i], o + q) for q in range(8)] for i in range(j + 1, n)]
            nc = list(raw[0])
        rk = [None] * 8
        fs = {}
        for k in range(8):
            rk[k] = 1.0 / m[k, k]
            for q in range(k + 1, 8):
                if q == k + 1:
                    m[q, q] = m[q, q] - (m[q, k] * m[q, k]) * rk[k]
                f = m[q, k] * rk[k]
                fs[q, k] = f
                for p in range(q + (1 if q == k + 1 else 0), 8):
                    m[p, q] = m[p, q] - m[p, k] * f
                rb[q] = rb[q] - f * rb[k]
                eb[q] = eb[q] - f * eb[k]
                if nxt:
                    nc[q] = nc[q] - f * nc[k]
            if nxt:
                c = nc[k] * rk[k]
                rows[j + 1] = rows[j + 1] - c * rb[k]
                eye[j + 1] = eye[j + 1] - c * eb[k]
        sk = lax.rsqrt(merge([m[k, k] for k in range(8)]))
        upper.append(merge(rb) * sk)
        inverse.append(merge(eb) * sk)
        if j + 2 < n:
            vr = [rb[k] * rk[k] for k in range(8)]
            ve = [eb[k] * rk[k] for k in range(8)]
            for q in range(7, -1, -1):
                for k in range(q):
                    vr[k] = vr[k] - fs[q, k] * vr[q]
                    ve[k] = ve[k] - fs[q, k] * ve[q]
            for i in range(j + 2, n):
                ar, ae = rows[i], eye[i]
                for q in range(8):
                    c = raw[i - j - 1][q]
                    ar = ar - c * vr[q]
                    ae = ae - c * ve[q]
                rows[i], eye[i] = ar, ae
    return jnp.concatenate(upper, 0), jnp.concatenate(inverse, 0)


def body(
    a_ref, m_ref, rbuf, cbuf, lw, dbuf, work, lref, wref, lh, ll, wh, wl, xh, xl, uh, ul,
    ssem, r1, r2, r3, r4, c0, c1, c2, c3, d1, d2, d3, d5, l4, tsem, lsem,
):
    row = lax.axis_index("row")
    col = lax.axis_index("col")
    h = lax.rem(row, 2)
    z = lax.div(row, 2)
    x = lax.div(col, 4)
    y = lax.rem(col, 4)
    major = jnp.where(h == 0, x, y)
    def put(src, dst, send, recv, row_to, col_to):
        return pltpu.make_async_remote_copy(
            src_ref=src, dst_ref=dst, send_sem=send, recv_sem=recv,
            device_id=(row_to, col_to), device_id_type=MESH,
        )

    def rows(start, size):
        return pl.ds(pl.multiple_of(start * size, size), size)

    barrier = pltpu.get_barrier_semaphore()

    def greet(row_to, col_to):
        pl.semaphore_signal(barrier, inc=1, device_id=(row_to, col_to), device_id_type=MESH)

    @pl.loop(1, 16)
    def _(t):
        greet(row, lax.rem(col + t, 16))
        greet(2 * z + 1 - h, lax.rem(col + t, 16))

    for t in range(1, 4):
        greet(2 * lax.rem(z + t, 4), col)
        greet(2 * lax.rem(z + t, 4) + 1, col)
    greet(2 * z + 1 - h, col)

    @pl.when((h == 0) & (x == 0))
    def _():
        @pl.loop(0, 32)
        def _(i):
            @pl.when((lax.div(i, 4) != row) | (lax.rem(i, 4) != col))
            def _():
                greet(lax.div(i, 4), lax.rem(i, 4))

    load = pltpu.make_async_copy(a_ref, m_ref, lsem.at[0, 2])
    load.start()

    @pl.when(h == 0)
    def _():
        lref[...] = jnp.zeros_like(lref)

    load.wait()
    @pl.when(x != 0)
    def _():
        pl.semaphore_wait(barrier, 37)

    @pl.when((x == 0) & (h == 0))
    def _():
        pl.semaphore_wait(barrier, 52)

    @pl.when((x == 0) & (h == 1))
    def _():
        pl.semaphore_wait(barrier, 53)

    def panel(p):
        first = 2 * p
        second = first + 1
        is_source = (x == 0) & ((y == first) | (y == second))
        root = (row == first) & (col == first)
        half = jnp.where(y == second, 1, 0)
        mycols = pl.ds(pl.multiple_of(half * T, T), T)
        scols = [pl.ds(0, T), pl.ds(T, T)]
        R, C, LW, D = rbuf.at[p], cbuf.at[p], lw.at[p], dbuf.at[p]
        other = 2 * z + 1 - h

        head = D.at[pl.ds(0, B), pl.ds(0, B)]
        parts = ((B, 24, T), (T, 32, W))

        def h_plane(t):
            return put(
                m_ref.at[pl.ds(0, B), pl.ds(0, B)], head, ssem.at[p, 5, t], d5.at[p, 0],
                row, lax.rem(col + t, 16),
            )

        def h_planes(t):
            return put(
                head, head, ssem.at[p, 2, t], d5.at[p, 1], 2 * lax.rem(z + t, 4) + h, col
            )

        def head_start():
            @pl.when(root)
            def _():
                @pl.loop(1, 16)
                def _(t):
                    h_plane(t).start()

                own = pltpu.make_async_copy(
                    m_ref.at[pl.ds(0, B), pl.ds(0, B)], head, lsem.at[p, 2]
                )
                own.start()
                own.wait()
                for t in (1, 2, 3):
                    h_planes(t).start()

        def head_wait():
            @pl.when(z == p)
            def _():
                @pl.when(jnp.logical_not(root))
                def _():
                    h_plane(1).wait_recv()
                    for t in (1, 2, 3):
                        h_planes(t).start()

            @pl.when(z != p)
            def _():
                h_planes(1).wait_recv()

        def d_rows(n, i, count=1):
            start, size, width = parts[n]
            return D.at[
                pl.ds(pl.multiple_of(start + i * size, 8), count * size), pl.ds(0, width)
            ]

        def d_scatter(n, i, s):
            start, size, _w = parts[n]
            here = pl.ds(pl.multiple_of((0 if n else start) + i * size, 8), size)
            there = pl.ds(pl.multiple_of(start + i * size, 8), size)
            return (
                m_ref.at[here, :], D.at[there, s if n else pl.ds(0, T)],
                ssem.at[p, n, i], d1.at[p, n + (half if n else 0)],
                2 * lax.div(i, 4), lax.rem(i, 4),
            )

        def d_source(n):
            return is_source & (row == second) if n else root

        def d_out(n, fn):
            @pl.loop(0, 16)
            def _(i):
                if n:
                    fn(put(*d_scatter(n, i, mycols)))
                else:
                    @pl.when(i != d_mine)
                    def _():
                        fn(put(*d_scatter(n, i, mycols)))

        d_mine = 4 * z + y

        def d_start(n):
            @pl.when(d_source(n))
            def _():
                d_out(n, lambda c: c.start())
                if n == 0:
                    src, dst = d_scatter(n, d_mine, mycols)[:2]
                    own = pltpu.make_async_copy(src, dst, lsem.at[p, 3])
                    own.start()
                    own.wait()

        def d_x(n, t):
            ref = d_rows(n, d_mine)
            return put(
                ref, ref, ssem.at[p, 3 + n, t], d2.at[p, n], row, 4 * lax.rem(x + t, 4) + y
            )

        def d_y(n, t):
            ref = d_rows(n, d_mine)
            return put(
                ref, ref, ssem.at[p, 6 + n, t], d3.at[p, n, t], row, 4 * x + lax.rem(y + t, 4)
            )

        def d_z(n, t):
            ref = d_rows(n, 4 * z, 4)
            return put(
                ref, ref, ssem.at[p, 6 + n, 4 + t], d3.at[p, n, 4 + t],
                2 * lax.rem(z + t, 4) + h, col,
            )

        def d_forward(n):
            @pl.when(x == 0)
            def _():
                for s in range(1 + n):
                    here = put(*d_scatter(n, d_mine, scols[s])[:3], d1.at[p, n + s], row, col)
                    if n:
                        here.wait_recv()
                    else:
                        pl.when(jnp.logical_not(root))(here.wait_recv)
                for t in (1, 3, 2):
                    d_x(n, t).start()

        def d_second(n):
            pl.when(x != 0)(d_x(n, 1).wait_recv)
            for t in (1, 3, 2):
                d_y(n, t).start()

        def d_third(n):
            for t in (1, 3, 2):
                ref = d_rows(n, 4 * z + lax.rem(y + 4 - t, 4))
                put(ref, ref, ssem.at[p, 6 + n, 0], d3.at[p, n, t], row, col).wait_recv()
            for t in (1, 3, 2):
                d_z(n, t).start()

        def d_gather(n):
            for t in (1, 3, 2):
                ref = d_rows(n, 4 * lax.rem(z + 4 - t, 4), 4)
                put(ref, ref, ssem.at[p, 6 + n, 0], d3.at[p, n, 4 + t], row, col).wait_recv()

        last_tile = lref.at[pl.ds(T, T), pl.ds(T, T)]

        def last_send():
            return put(last_tile, last_tile, ssem.at[p, 8, 5], tsem.at[p], other, col)

        def r_place(q):
            return (x, y) if q == 0 else (y, x)

        def r_col(q, ma, mi):
            return 4 * ma + mi if q == 0 else 4 * mi + ma

        def r_scatter(i):
            to = jnp.where(h == 0, i, 4 * lax.rem(i, 4) + lax.div(i, 4))
            return put(
                m_ref.at[rows(i, 64), :], R.at[h, rows(i, 64), mycols],
                ssem.at[p, 13, i], r1.at[p, h, half], 2 * z + 1, to,
            )

        def r_own(fn):
            @pl.loop(0, 16)
            def _(i):
                @pl.when((h == 0) | (i != 4 * y + x))
                def _():
                    fn(i)

        def r_piece(q, ma, mi):
            return R.at[q, rows(4 * ma + mi, 64), :]

        def r_minor(q, t):
            ma, mi = r_place(q)
            ref = r_piece(q, ma, mi)
            return put(
                ref, ref, ssem.at[p, 16 + q, t - 1], r2.at[p, q, t - 1],
                row, r_col(q, ma, lax.rem(mi + t, 4)),
            )

        def r_minor_in(q, t):
            ma, mi = r_place(q)
            ref = r_piece(q, ma, lax.rem(mi + 4 - t, 4))
            put(ref, ref, ssem.at[p, 16, 0], r2.at[p, q, t - 1], row, col).wait_recv()

        def r_major(q, slot, t):
            ma, mi = r_place(q)
            ref = r_piece(q, ma, lax.rem(mi + 4 - slot, 4))
            return put(
                ref, ref, ssem.at[p, 16 + q, 3 + 3 * slot + t - 1], r3.at[p, q, 3 * slot + t - 1],
                row, r_col(q, lax.rem(ma + t, 4), mi),
            )

        def r_major_in(q, t):
            ma, mi = r_place(q)
            for slot in range(4):
                ref = r_piece(q, lax.rem(ma + 4 - t, 4), lax.rem(mi + 4 - slot, 4))
                put(
                    ref, ref, ssem.at[p, 16, 0], r3.at[p, q, 3 * slot + t - 1], row, col
                ).wait_recv()

        def r_core(t):
            ref = R.at[0, rows(lax.rem(x + 4 - t, 4), 256), :]
            return put(ref, ref, ssem.at[p, 18, t], r4.at[p, t], 2 * z, col)

        def r_first():
            for q in range(2):
                for s in range(2):
                    there = put(
                        m_ref.at[rows(0, 64), :], R.at[q, rows(0, 64), scols[s]],
                        ssem.at[p, 13, 0], r1.at[p, q, s], row, col,
                    )
                    if q == 0:
                        there.wait_recv()
                    else:
                        pl.when(jnp.logical_not((x == 0) & (y == first + s)))(there.wait_recv)
                for t in (1, 3, 2):
                    r_minor(q, t).start()
                for t in (1, 3, 2):
                    r_major(q, 0, t).start()

        def r_second():
            for slot in (1, 3, 2):
                for q in range(2):
                    r_minor_in(q, slot)
                    for t in (1, 3, 2):
                        r_major(q, slot, t).start()

        def c_rows(hh, q):
            return pl.ds(pl.multiple_of(hh * T + q * B, B), B)

        def c_tile(hh):
            return C.at[pl.ds(pl.multiple_of(hh * T, T), T), :]

        def c_first(hh, t, which):
            zt = lax.rem(z + t, 4)
            ref = C.at[c_rows(hh, zt if which == 0 else z), :]
            return put(
                ref, ref, ssem.at[p, 15, 6 * hh + 2 * (t - 1) + which], c1.at[p, hh, which],
                2 * zt + 1, col,
            )

        def c_first_in(hh, which):
            ref = C.at[c_rows(hh, z if which == 0 else p), :]
            put(ref, ref, ssem.at[p, 15, 0], c1.at[p, hh, which], row, col).wait_recv()

        def c_second(hh, t):
            ref = C.at[c_rows(hh, z), :]
            return put(
                ref, ref, ssem.at[p, 14, 3 * hh + t - 1], c2.at[p, hh, t - 1],
                2 * lax.rem(z + t, 4) + 1, col,
            )

        def c_second_in(hh, t):
            ref = C.at[c_rows(hh, lax.rem(z + 4 - t, 4)), :]
            put(ref, ref, ssem.at[p, 14, 0], c2.at[p, hh, t - 1], row, col).wait_recv()

        def c_sibling():
            return put(
                m_ref.at[pl.ds(0, T), :], c_tile(0), ssem.at[p, 8, 7], c0.at[p], other, col
            )

        def c_core():
            return put(C, C, ssem.at[p, 8, 6], c3.at[p], other, col)

        def c_start():
            @pl.when((z == p) & (h == 1))
            def _():
                own = pltpu.make_async_copy(
                    m_ref.at[pl.ds(0, T), :], c_tile(1), lsem.at[p, 1]
                )
                own.start()
                own.wait()
                for hh in (1, 0):
                    if hh == 0:
                        c_sibling().wait_recv()
                    for t in (1, 3, 2):
                        for which in (0, 1):
                            c_first(hh, t, which).start()

        def c_forward():
            @pl.when(z != p)
            def _():
                for hh in range(2):
                    c_first_in(hh, 0)
                    for t in (1, 2, 3):
                        @pl.when(lax.rem(z + t, 4) != p)
                        def _():
                            c_second(hh, t).start()

        def c_cross():
            @pl.when(z != p)
            def _():
                for hh in range(2):
                    c_first_in(hh, 1)
                    for t in (1, 2, 3):
                        @pl.when(lax.rem(z + 4 - t, 4) != p)
                        def _():
                            c_second_in(hh, t)

        def l_core(g):
            ref = LW.at[pl.ds(g * H, W - g * H), pl.ds(g * H, H)]
            return put(ref, ref, ssem.at[p, 8, 1 + g], l4.at[p, g], other, col)

        d_start(0)
        head_start()
        d_start(1)

        @pl.when((z == p) & (h == 0))
        def _():
            c_sibling().start()

        @pl.when(is_source)
        def _():
            r_own(lambda i: r_scatter(i).start())

            @pl.when(h == 1)
            def _():
                own = pltpu.make_async_copy(
                    m_ref.at[rows(4 * y + x, 64), :],
                    R.at[1, rows(4 * y + x, 64), mycols], lsem.at[p, 0],
                )
                own.start()
                own.wait()

        def close(g, w0, l10, w1):
            low = dot3(split(w1), split(dot3(split(l10), split(w0), NN)), NN)
            big = jnp.concatenate(
                [
                    jnp.concatenate([w0, jnp.zeros_like(w0)], 1),
                    jnp.concatenate([-low, w1], 1),
                ],
                0,
            )
            wh[g], wl[g] = split(big)
            return big

        right_of = col > second
        in_panel = (col == first) | (col == second)
        top_below = row > second
        top_band = (row == first) | (row == second)
        column_half = jnp.where(col == second, 1, 0)

        def absorb(g):
            ds = pl.ds(g * H, H)
            wh[g], wl[g] = split(LW[ds, ds])
            for j in range(g + 1, 4):
                js = pl.ds(j * H, H)
                lh[js, ds], ll[js, ds] = split(LW[js, ds])

        def block(i):
            return pl.ds(i * H, H)

        def u_value(kb, cs):
            ks, done = block(kb), pl.ds(0, kb * H)
            value = C[ks, cs]
            if kb:
                value = value - dot3(
                    (lh[ks, done], ll[ks, done]), (uh[done, cs], ul[done, cs]), NN
                )
            return value

        def u_step(kb, ready=False):
            for n in range(2):
                cs = block(n)
                value = C[block(kb), cs] if ready else u_value(kb, cs)
                uk = dot3((wh[kb], wl[kb]), split(value), NN)
                uh[block(kb), cs], ul[block(kb), cs] = split(uk)
                if not ready:
                    C[block(kb), cs] = uk

        def u_ahead():
            for n in range(2):
                C[block(3), block(n)] = u_value(3, block(n))

        def x_value(q, g, kb):
            rs, ks, done = rows(g, H), block(kb), pl.ds(0, kb * H)
            value = R[q, rs, ks]
            if kb:
                value = value - dot3(
                    (xh[rs, done], xl[rs, done]), (lh[ks, done], ll[ks, done])
                )
            return value

        def keep_x(g, kb, xk):
            @pl.when(((g >= 2) | top_below) & in_panel & (column_half == kb // 2))
            def _():
                m_ref[rows(g, H), pl.ds(kb % 2 * H, H)] = xk

        def x_group(q, g):
            rs = rows(g, H)
            for kb in range(3):
                xk = dot3(split(x_value(q, g, kb)), (wh[kb], wl[kb]))
                xh[rs, block(kb)], xl[rs, block(kb)] = split(xk)
                if q:
                    keep_x(g, kb, xk)
                else:
                    R[q, rs, block(kb)] = xk
            R[q, rs, block(3)] = x_value(q, g, 3)

        def x_last(g):
            rs = rows(g, H)
            xk = dot3(split(R[h, rs, block(3)]), (wh[3], wl[3]))
            xh[rs, block(3)], xl[rs, block(3)] = split(xk)
            keep_x(g, 3, xk)

        def update(g):
            @pl.when(((g >= 2) | top_below) & right_of)
            def _():
                rs = rows(g, H)
                for n in range(2):
                    cs = pl.ds(n * H, H)
                    m_ref[rs, cs] = m_ref[rs, cs] - dot3(
                        (xh[rs, :], xl[rs, :]), (uh[:, cs], ul[:, cs]), NN
                    )

        def both(kb):
            u_step(kb)
            x_step(major, kb)

        def drain_source():
            for n in range(2):
                @pl.when(d_source(n))
                def _():
                    d_out(n, lambda c: c.wait_send())

            @pl.when(root)
            def _():
                @pl.loop(1, 16)
                def _(t):
                    h_plane(t).wait_send()

            @pl.when(is_source)
            def _():
                r_own(lambda i: r_scatter(i).wait_send())

            @pl.when((z == p) & (h == 1))
            def _():
                for hh in range(2):
                    for t in (1, 2, 3):
                        for which in (0, 1):
                            c_first(hh, t, which).wait_send()

            @pl.when((z == p) & (h == 0))
            def _():
                c_sibling().wait_send()

        def drain_r():
            for q in range(2):
                for t in (1, 2, 3):
                    r_minor(q, t).wait_send()
                    for slot in range(4):
                        r_major(q, slot, t).wait_send()

        def drain_c():
            @pl.when(z != p)
            def _():
                for t in (1, 2, 3):
                    @pl.when(lax.rem(z + t, 4) != p)
                    def _():
                        for hh in range(2):
                            c_second(hh, t).wait_send()

        @pl.when(h == 0)
        def _():
            head_wait()
            d_forward(0)
            d_forward(1)
            d_second(0)
            d_third(0)
            d_second(1)
            work[0:B, 0:B] = D[0:B, 0:B]

            def keep(rs, cs, value, tile=True):
                if tile:
                    lref[rs, cs] = value
                LW[rs, cs] = value
                pair_ = split(value)
                lh[rs, cs], ll[rs, cs] = pair_
                return pair_

            def close_root(g):
                s0, s1 = slice(g * H, g * H + B), slice(g * H + B, g * H + H)
                big = close(g, wref[s0, :], lref[s1, s0], wref[s1, :])
                LW[g * H : g * H + H, g * H : g * H + H] = big
                return wh[g], wl[g]

            def send(g):
                l_core(g).start()

            @pl.loop(0, W // B)
            def _(k):
                q0, q1, q2, q3 = (slice(i * H, i * H + H) for i in range(4))

                @pl.when(k == 1)
                def _():
                    d_third(1)
                    d_gather(0)
                    work[B:H, 0:H] = D[B:H, 0:H]

                @pl.when(k == 2)
                def _():
                    w = close_root(0)
                    xs = keep(q1, q0, dot3(split(D[q1, q0]), w))
                    work[q1, q1] = D[q1, q1] - dot3(xs, xs)

                @pl.when(k == 4)
                def _():
                    w = close_root(1)
                    d_gather(1)
                    es = keep(slice(T, W), q0, dot3(split(D[T:W, q0]), (wh[0], wl[0])), False)
                    send(0)
                    rest = D[T:W, q1] - dot3(es, (lh[q1, q0], ll[q1, q0]))
                    keep(slice(T, W), q1, dot3(split(rest), w), False)
                    send(1)
                    left = lambda r: (lh[r, 0:T], ll[r, 0:T])
                    work[q2, q2] = D[q2, q2] - dot3(left(q2), left(q2))
                    work[q3, q2] = D[q3, q2] - dot3(left(q3), left(q2))
                    work[q3, q3] = D[q3, q3] - dot3(left(q3), left(q3))

                @pl.when(k == 6)
                def _():
                    w = close_root(2)
                    xs = keep(q3, q2, dot3(split(work[q3, q2]), w))
                    send(2)
                    work[q3, q3] = work[q3, q3] - dot3(xs, xs)

                o = pl.multiple_of(k * B, B)
                here = pl.ds(o, B)
                before = pl.ds(pl.multiple_of(jnp.maximum(o - B, 0), B), B)

                @pl.when(lax.rem(k, 2) == 1)
                def _():
                    xk = dot3(split(work[here, before]), split(wref[before, :]))
                    lref[here, before] = xk
                    xs = split(xk)
                    work[here, here] = work[here, here] - dot3(xs, xs)

                upper, inverse = chol_block(work[here, here])
                wref[here, :] = inverse

                @pl.when((row == first) & in_panel)
                def _():
                    ri = lax.broadcasted_iota(jnp.int32, (B, B), 0)
                    ci = lax.broadcasted_iota(jnp.int32, (B, B), 1)
                    lref[here, here] = jnp.where(ri >= ci, upper.T, 0.0)

            close_root(3)
            l_core(3).start()

            @pl.when((row == first) & (col == second))
            def _():
                last_send().start()

            drain_source()
            c_core().wait_recv()
            for kb in range(3):
                uh[block(kb), :], ul[block(kb), :] = split(C[block(kb), :])
            for t in range(4):
                r_core(t).wait_recv()

            @pl.loop(0, 4)
            def _(g):
                rs = rows(g, H)
                for kb in range(3):
                    xk = R[0, rs, block(kb)]
                    xh[rs, block(kb)], xl[rs, block(kb)] = split(xk)
                    keep_x(g, kb, xk)

        @pl.when(h == 1)
        def _():
            c_start()
            r_first()
            c_forward()
            r_second()
            c_cross()
            drain_source()
            drain_c()
            for kb in range(3):
                l_core(kb).wait_recv()
                absorb(kb)
                u_step(kb)
            u_ahead()
            c_core().start()
            for q in range(2):
                for t in (1, 3, 2):
                    r_major_in(q, t)
            drain_r()

            @pl.loop(0, 4)
            def _(t):
                g = lax.rem(x + 4 - t, 4)
                x_group(0, g)
                r_core(t).start()

            @pl.loop(0, 4)
            def _(g):
                x_group(1, g)

            l_core(3).wait_recv()
            absorb(3)

        u_step(3, True)

        @pl.loop(0, 4)
        def _(g):
            x_last(g)
            update(g)

        @pl.when(top_band & right_of)
        def _():
            m_ref[0:T, :] = jnp.zeros((T, T), jnp.float32)

        @pl.when(top_band & in_panel)
        def _():
            @pl.when(root)
            def _():
                m_ref[0:T, :] = lref[0:T, 0:T]

            @pl.when((row == first) & (col == second))
            def _():
                m_ref[0:T, :] = jnp.zeros((T, T), jnp.float32)

            @pl.when((row == second) & (col == first))
            def _():
                m_ref[0:T, :] = LW[T:W, 0:T]

            @pl.when((row == second) & (col == second))
            def _():
                last_send().wait_recv()
                m_ref[0:T, :] = last_tile[...]

        @pl.when(h == 1)
        def _():
            for t in range(4):
                r_core(t).wait_send()

        @pl.when(h == 1)
        def _():
            c_core().wait_send()

        @pl.when(h == 0)
        def _():
            for n in range(2):
                for t in (1, 3, 2):
                    d_y(n, t).wait_send()
                    d_z(n, t).wait_send()

                @pl.when(x == 0)
                def _():
                    for t in (1, 3, 2):
                        d_x(n, t).wait_send()

            for g in range(4):
                l_core(g).wait_send()

            @pl.when(z == p)
            def _():
                for t in (1, 2, 3):
                    h_planes(t).wait_send()

            @pl.when((row == first) & (col == second))
            def _():
                last_send().wait_send()

    pl.loop(0, 2)(panel)


def local(kernel):
    f32, b16 = jnp.float32, jnp.bfloat16
    dma = pltpu.SemaphoreType.DMA
    return pl.pallas_call(
        body,
        out_shape=jax.ShapeDtypeStruct((W, T), f32),
        in_specs=[pl.BlockSpec(memory_space=pl.ANY)],
        out_specs=pl.BlockSpec(memory_space=pltpu.VMEM),
        scratch_shapes=[
            pltpu.VMEM((2, 2, W, W), f32),
            pltpu.VMEM((2, W, T), f32),
            pltpu.VMEM((2, W, W), f32),
            pltpu.VMEM((2, W, W), f32),
            pltpu.VMEM((W, W), f32),
            pltpu.VMEM((W, W), f32),
            pltpu.VMEM((W, B), f32),
            pltpu.VMEM((W, W), b16),
            pltpu.VMEM((W, W), b16),
            pltpu.VMEM((4, H, H), b16),
            pltpu.VMEM((4, H, H), b16),
            pltpu.VMEM((W, W), b16),
            pltpu.VMEM((W, W), b16),
            pltpu.VMEM((W, T), b16),
            pltpu.VMEM((W, T), b16),
            dma((2, 19, 16)),
            dma((2, 2, 2)), dma((2, 2, 3)), dma((2, 2, 12)), dma((2, 4)),
            dma((2,)), dma((2, 2, 2)), dma((2, 2, 3)), dma((2,)),
            dma((2, 3)), dma((2, 2)), dma((2, 2, 12)), dma((2, 2)),
            dma((2, 4)),
            dma((2,)),
            dma((2, 4)),
        ],
        compiler_params=pltpu.CompilerParams(
            collective_id=0, has_side_effects=True, vmem_limit_bytes=62 * 1024 * 1024
        ),
        cost_estimate=pl.CostEstimate(
            flops=20_000_000_000, bytes_accessed=8_000_000, transcendentals=0
        ),
        name="two_panels",
    )(kernel)


def solution(mesh):
    return jax.shard_map(
        local,
        mesh=mesh,
        in_specs=(P("row", "col"),),
        out_specs=P("row", "col"),
        check_vma=False,
    )
```
